32 devices in a mesh: section: 4 (over x, core), dp: 8 (over z, y).
Axes of the slice: x: 2, y: 2, z: 4, core: 2. Of those that a mesh axis runs over, the one named last changes fastest.
Arguments:
- arriving_activations: bfloat16 [4, 16, 12, 12, 256], P('section', 'dp'), may hold values from -6 to 6
- fresh_images: bfloat16 [3, 16, 12, 12, 256], P(None, 'dp'), may hold values from -6 to 6
- saved_inputs: bfloat16 [4, 4, 16, 12, 12, 256], P(None, 'section', 'dp'), may hold values from -6 to 6
- arriving_gradients: bfloat16 [4, 16, 12, 12, 256], P('section', 'dp'), may hold values from -6 to 6
- fresh_gradients: bfloat16 [3, 16, 12, 12, 256], P(None, 'dp'), may hold values from -6 to 6
- feed_order: int32 [3], replicated, may hold values from 0 to 2, each once
- forward_weight: bfloat16 [4, 2304, 256], P('section'), may hold values from -0.125 to 0.125
- forward_gain: float32 [4, 256], P('section'), may hold values from 0.1 to 1.9
- forward_bias: float32 [4, 256], P('section'), may hold values from -3 to 3
- backward_weight: bfloat16 [4, 2304, 256], P('section'), may hold values from -0.125 to 0.125
- backward_gain: float32 [4, 256], P('section'), may hold values from 0.1 to 1.9
- backward_bias: float32 [4, 256], P('section'), may hold values from -3 to 3
Outputs:
- section_outputs: float32 [4, 4, 16, 12, 12, 256], P(None, 'section', 'dp')
- input_gradients: float32 [4, 4, 16, 12, 12, 256], P(None, 'section', 'dp')
- weight_gradient: float32 [4, 2304, 256], P('section', 'dp')
The draws below stay inside these ranges and needn't reach their ends.
Inputs may be any that keep to these rules, and one draw needn't show every extreme that they name: `feed_order`: each of 0 to 2 appears once.
All inputs are finite; a program needn't handle non-finite values.
Results may differ from the reference program's by a relative error of at most 0.0044.
Values sent between devices are 32-bit elements; how exact they have to be, the bound alone decides.
No kernel may reach another device: no remote copies, remote signals or barrier semaphores. Data moves between devices by JAX's collectives and lax.ppermute only.
A program may use at most 64 MiB of HBM per device.

```python
import jax
import jax.numpy as jnp
from jax import lax

C = 256
GROUPS = 32
HH = 12
WW = 12
TICKS = 4
BATCH = 16
N_LAYERS = 4


def levels(rng, extent, split, smallest, high):
    def one(position, blocks):
        steps = jax.random.uniform(jax.random.fold_in(jax.random.fold_in(rng, 6), position), (blocks,), jnp.float32, smallest / len(split), high / len(split))
        return jnp.repeat(jnp.exp(steps), extent[position] // blocks).reshape((-1,) + (1,) * (len(extent) - position - 1))

    loudness = one(*split[0])
    for cut in split[1:]:
        loudness = loudness * one(*cut)
    return loudness


def centred(key, shape, width, reach, shards=(), kind=jnp.bfloat16):
    values = width * jax.random.normal(key, shape, jnp.float32)
    if shards:
        values = values * levels(key, shape, shards, -0.22, 0.18)
    return jnp.clip(values, -reach, reach).astype(kind)


def setup_inputs(seed: int = 0) -> dict:
    keys = jax.random.split(jax.random.key(seed), 13)
    return {
        "arriving_activations": centred(keys[0], (N_LAYERS, BATCH, HH, WW, C), 1.0, 6.0, ((0, 4), (1, 8))),
        "fresh_images": centred(keys[1], (TICKS - 1, BATCH, HH, WW, C), 1.0, 6.0, ((1, 8),)),
        "saved_inputs": centred(keys[2], (TICKS, N_LAYERS, BATCH, HH, WW, C), 1.0, 6.0, ((1, 4), (2, 8))),
        "arriving_gradients": centred(keys[3], (N_LAYERS, BATCH, HH, WW, C), 1.0, 6.0, ((0, 4), (1, 8))),
        "fresh_gradients": centred(keys[4], (TICKS - 1, BATCH, HH, WW, C), 1.0, 6.0, ((1, 8),)),
        "feed_order": jax.random.permutation(keys[5], TICKS - 1).astype(jnp.int32),
        "forward_weight": centred(keys[6], (N_LAYERS, 9 * C, C), (9 * C) ** -0.5, 0.125, ((0, 4),)),
        "forward_gain": jnp.clip(1.0 + 0.18 * jax.random.normal(keys[7], (N_LAYERS, C), jnp.float32), 0.1, 1.9),
        "forward_bias": centred(keys[8], (N_LAYERS, C), 0.5, 3.0, ((0, 4),), jnp.float32),
        "backward_weight": centred(keys[9], (N_LAYERS, 9 * C, C), (9 * C) ** -0.5, 0.125, ((0, 4),)),
        "backward_gain": jnp.clip(1.0 + 0.18 * jax.random.normal(keys[10], (N_LAYERS, C), jnp.float32), 0.1, 1.9),
        "backward_bias": centred(keys[11], (N_LAYERS, C), 0.5, 3.0, ((0, 4),), jnp.float32),
    }


def group_norm_silu(values, gain, bias):
    grouped = values.reshape(values.shape[0], values.shape[1] * values.shape[2], GROUPS, -1)
    average = lax.optimization_barrier(jnp.mean(grouped, axis=(1, 3), keepdims=True))
    spread = lax.optimization_barrier(jnp.mean(jnp.square(grouped - average), axis=(1, 3), keepdims=True))
    normed = ((grouped - average) * lax.rsqrt(spread + 1e-05)).reshape(values.shape)
    scaled = normed * gain + bias
    return scaled * jax.nn.sigmoid(scaled)

def patches(images):
    rows = images.shape[1]
    cols = images.shape[2]
    padded = jnp.pad(images, ((0, 0), (1, 1), (1, 1), (0, 0)))
    shifted = [padded[:, shift_row:shift_row + rows, shift_col:shift_col + cols, :] for shift_row in range(3) for shift_col in range(3)]
    return jnp.concatenate(shifted, axis=-1).reshape(-1, 9 * images.shape[3])

def flipped(weight):
    channels = weight.shape[1]
    return weight.reshape(3, 3, channels, channels)[::-1, ::-1].transpose(0, 1, 3, 2).reshape(9 * channels, channels)

def forward_layer(inputs, weight, gain, bias):
    widened = inputs.astype(jnp.float32)
    hidden = group_norm_silu(widened, gain, bias).astype(jnp.bfloat16)
    convolved = jnp.dot(patches(hidden), weight, preferred_element_type=jnp.float32).reshape(inputs.shape)
    return widened + convolved

def backward_layer(saved, incoming, weight, gain, bias):
    widened = saved.astype(jnp.float32)
    activated, pullback = jax.vjp(lambda values: group_norm_silu(values, gain, bias), widened)
    hidden = activated.astype(jnp.bfloat16)
    narrow = incoming.astype(jnp.bfloat16)
    hidden_grad = jnp.dot(patches(narrow), flipped(weight), preferred_element_type=jnp.float32).reshape(saved.shape)
    through_norm, = pullback(hidden_grad)
    gradient = incoming.astype(jnp.float32) + through_norm
    incoming_rows = narrow.reshape(-1, narrow.shape[3])
    term = lax.dot_general(patches(hidden), incoming_rows, (((0,), (0,)), ((), ())), preferred_element_type=jnp.float32)
    return (gradient, term)

def reference(arriving_activations, fresh_images, saved_inputs, arriving_gradients, fresh_gradients, feed_order, forward_weight, forward_gain, forward_bias, backward_weight, backward_gain, backward_bias):
    act_in = arriving_activations.astype(jnp.float32)
    grad_in = arriving_gradients.astype(jnp.float32)
    emitted = []
    returned = []
    weight_total = jnp.zeros(backward_weight.shape, jnp.float32)
    act_out = act_in
    grad_out = grad_in
    for tick_num in range(TICKS):
        if tick_num > 0:
            index = feed_order[tick_num - 1].astype(jnp.int32)
            chosen = lax.dynamic_index_in_dim(fresh_images, index, 0, keepdims=True).astype(jnp.float32)
            act_in = jnp.concatenate([chosen, act_out[:-1]], axis=0)
            chosen_grad = lax.dynamic_index_in_dim(fresh_gradients, index, 0, keepdims=True).astype(jnp.float32)
            grad_in = jnp.concatenate([chosen_grad, grad_out[:-1]], axis=0)
        act_out = lax.map(lambda packed: forward_layer(*packed), (act_in, forward_weight, forward_gain, forward_bias))
        grad_out, terms = lax.map(lambda packed: backward_layer(*packed), (saved_inputs[tick_num], grad_in, backward_weight, backward_gain, backward_bias))
        weight_total = weight_total + terms
        emitted.append(act_out)
        returned.append(grad_out)
    return (jnp.stack(emitted), jnp.stack(returned), weight_total * (1.0 / BATCH))
```

```python
import functools
import math

import jax
import jax.numpy as jnp
from jax import lax
from jax.experimental import pallas as pl
from jax.experimental.pallas import tpu as pltpu
from jax.sharding import PartitionSpec as P

GROUPS = 32
F32 = jnp.float32
BF16 = jnp.bfloat16
LANES = 128
VMEM_LIMIT = 24 * 1024 * 1024


class Dims:
    def __init__(self, images, rows, cols, channels):
        self.n, self.h, self.w, self.c = images, rows, cols, channels
        self.cts = channels // LANES
        self.unit = self.cts * images
        self.pix = rows * cols
        self.flat = self.pix * self.unit
        per = 8 // math.gcd(8, self.unit)
        self.pad = -(-(cols + 1) // per) * per
        self.padded = (self.pix + 2 * self.pad) * self.unit
        self.count = self.pix * (channels // GROUPS)


def interleaved(x, d):
    lead = x.shape[:-4]
    k = len(lead)
    x = x.reshape(*lead, d.n, d.pix, d.cts, LANES)
    x = x.transpose(*range(k), k + 1, k + 2, k, k + 3)
    return x.reshape(*lead, d.flat, LANES)


def standard(x, d):
    lead = x.shape[:-2]
    k = len(lead)
    x = x.reshape(*lead, d.pix, d.cts, d.n, LANES)
    x = x.transpose(*range(k), k + 2, k, k + 1, k + 3)
    return x.reshape(*lead, d.n, d.h, d.w, d.c)


def group_sum(v, width):
    lane = lax.broadcasted_iota(jnp.int32, v.shape, 1)
    k = 1
    while k < width:
        v = v + jnp.where((lane & k) == 0, pltpu.roll(v, LANES - k, 1), pltpu.roll(v, k, 1))
        k *= 2
    return v


def pattern(ref, d):
    row = lax.broadcasted_iota(jnp.int32, (8, LANES), 0)
    ct = (row // d.n) % d.cts
    out = jnp.broadcast_to(ref[0:1, :], (8, LANES))
    for i in range(1, d.cts):
        out = jnp.where(ct == i, jnp.broadcast_to(ref[i : i + 1, :], (8, LANES)), out)
    return out


def unit_sum(v, d):
    s = jnp.sum(v, axis=0)
    k = d.unit
    while k < 8:
        s = s + pltpu.roll(s, k, 0)
        k *= 2
    return group_sum(s, d.c // GROUPS)


def normalized(x, d):
    tiles = x.reshape(-1, 8, LANES)
    scale = 1.0 / d.count
    mean = unit_sum(tiles, d) * scale
    centred = tiles - mean
    var = unit_sum(centred * centred, d) * scale
    rstd = lax.rsqrt(var + 1e-05)
    return centred * rstd, rstd


def sigmoid(a):
    return 0.5 * jnp.tanh(0.5 * a) + 0.5


def spread(value, refs, d):
    zeros = jnp.zeros((d.pad * d.unit, LANES), F32)
    for ref in refs:
        ref[0 : d.pad * d.unit, :] = zeros
        ref[d.padded - d.pad * d.unit : d.padded, :] = zeros
        ref[d.pad * d.unit : d.pad * d.unit + d.flat, :] = value
    edge = jnp.zeros((d.unit, LANES), F32)
    for i in range(d.h):
        last = (d.pad + i * d.w + d.w - 1) * d.unit
        first = (d.pad + i * d.w) * d.unit
        refs[0][last : last + d.unit, :] = edge
        refs[2][first : first + d.unit, :] = edge


def plane(ref, d, shift, n):
    parts = [
        ref[pl.ds((d.pad + shift) * d.unit + ct * d.n + n, d.pix, stride=d.unit), :] for ct in range(d.cts)
    ]
    return jnp.concatenate(parts, axis=1)


def gather_patches(refs, out_ref, d):
    for kr in range(3):
        for kc in range(3):
            tap = kr * 3 + kc
            for n in range(d.n):
                block = plane(refs[kc], d, (kr - 1) * d.w + kc - 1, n)
                out_ref[n * d.pix : (n + 1) * d.pix, tap * d.c : (tap + 1) * d.c] = block.astype(BF16)


def from_interleaved(ref, d, base=0):
    rows = [
        jnp.concatenate(
            [ref[pl.ds(base + ct * d.n + n, d.pix, stride=d.unit), :] for ct in range(d.cts)], axis=1
        )
        for n in range(d.n)
    ]
    return jnp.concatenate(rows, axis=0)


def to_interleaved(ref, n, value, d):
    for ct in range(d.cts):
        ref[pl.ds(ct * d.n + n, d.pix, stride=d.unit), :] = value[:, ct * LANES : (ct + 1) * LANES]


def prep_kernel(d, saved_ref, gain_ref, bias_ref, slope_ref, normed_ref, rstd_ref, hidden_ref, tmp):
    x = saved_ref[...].astype(F32)
    normed, rstd = normalized(x, d)
    gain = pattern(gain_ref, d)
    a = normed * gain + pattern(bias_ref, d)
    s = sigmoid(a)
    rstd_ref[...] = rstd
    for ref, value in (
        (normed_ref, normed),
        (slope_ref, s * (1.0 + a * (1.0 - s)) * gain),
        (hidden_ref, a * s),
    ):
        tmp[...] = value.reshape(d.flat, LANES)
        ref[...] = from_interleaved(tmp, d).astype(ref.dtype)


def entering(first, sec_ref, fresh_ref, arrived_ref):
    fresh = fresh_ref[0].astype(F32)
    if first:
        return fresh
    return jnp.where(sec_ref[1] == 0, fresh, arrived_ref[...])


def backward_kernel(
    d, first, sec_ref, fresh_ref, arrived_ref, slope_ref, normed_ref, rstd_ref, weight_ref, out_ref, e_ref, left, mid, right, cols
):
    e = entering(first, sec_ref, fresh_ref, arrived_ref)
    e_ref[...] = e
    spread(e, (left, mid, right), d)
    gather_patches((left, mid, right), cols, d)
    grad = None
    for tap in range(9):
        part = lax.dot_general(
            cols[:, tap * d.c : (tap + 1) * d.c],
            weight_ref[(8 - tap) * d.c : (9 - tap) * d.c, :],
            (((1,), (1,)), ((), ())),
            preferred_element_type=F32,
        )
        grad = part if grad is None else grad + part
    through = grad * slope_ref[...]
    weighted = through * normed_ref[...]
    rows = []
    for ct in range(d.cts):
        for n in range(d.n):
            for v in (through, weighted):
                rows.append(
                    jnp.sum(v[n * d.pix : (n + 1) * d.pix, ct * LANES : (ct + 1) * LANES], axis=0, keepdims=True)
                )
    sums = group_sum(jnp.concatenate(rows, axis=0), d.c // GROUPS) * (1.0 / d.count)
    for n in range(d.n):
        for ct in range(d.cts):
            k = (ct * d.n + n) * 2
            here = (slice(n * d.pix, (n + 1) * d.pix), slice(ct * LANES, (ct + 1) * LANES))
            rstd = rstd_ref[ct * d.n + n : ct * d.n + n + 1, :]
            value = (through[here] - sums[k : k + 1] - normed_ref[here] * sums[k + 1 : k + 2]) * rstd
            where = ct * d.n + n
            e_here = mid[pl.ds(d.pad * d.unit + where, d.pix, stride=d.unit), :]
            out_ref[pl.ds(where, d.pix, stride=d.unit), :] = value + e_here


def forward_kernel(
    d, first, sec_ref, fresh_ref, arrived_ref, gain_ref, bias_ref, weight_ref, out_ref, left, mid, right, cols, kept
):
    x = entering(first, sec_ref, fresh_ref, arrived_ref)
    kept[...] = x
    normed, _ = normalized(x, d)
    a = normed * pattern(gain_ref, d) + pattern(bias_ref, d)
    hidden = (a * sigmoid(a)).reshape(d.flat, LANES)
    spread(hidden, (left, mid, right), d)
    gather_patches((left, mid, right), cols, d)
    conv = jnp.dot(cols[...], weight_ref[...], preferred_element_type=F32)
    for n in range(d.n):
        for ct in range(d.cts):
            where = pl.ds(ct * d.n + n, d.pix, stride=d.unit)
            out_ref[where, :] = (
                kept[where, :] + conv[n * d.pix : (n + 1) * d.pix, ct * LANES : (ct + 1) * LANES]
            )


def weight_kernel(d, ticks, chunk, factor, slot_ref, *refs):
    e_refs, h_refs = refs[:ticks], refs[ticks : 2 * ticks]
    up_ref, down_ref, left, mid, right, cols, hid = refs[2 * ticks :]
    rows = d.n * d.pix
    for t in range(ticks):
        spread(e_refs[t][...], (left, mid, right), d)
        gather_patches((left, mid, right), cols.at[t * rows : (t + 1) * rows], d)
        hid[t * rows : (t + 1) * rows, :] = h_refs[t][...]
    h = hid[...]
    size = math.gcd(d.c, chunk)
    for tap in range(9):
        block = lax.dot_general(
            h, cols[:, (8 - tap) * d.c : (9 - tap) * d.c], (((0,), (0,)), ((), ())), preferred_element_type=F32
        ) * factor
        at = tap * d.c
        while at < (tap + 1) * d.c:
            owner = at // chunk
            stop = min((owner + 1) * chunk, (tap + 1) * d.c)
            piece = block[at - tap * d.c : stop - tap * d.c]
            where = pl.ds(at - owner * chunk, stop - at)
            up_ref[slot_ref[owner], where, :] = piece[:, :LANES]
            down_ref[slot_ref[owner + 9 * d.c // chunk], where, :] = piece[:, LANES:]
            at = stop


def call(body, out_shape, scratch, cost, *operands):
    smem = pl.BlockSpec(memory_space=pltpu.SMEM)
    vmem = pl.BlockSpec(memory_space=pltpu.VMEM)
    specs = [smem if o.dtype == jnp.int32 else vmem for o in operands]
    return pl.pallas_call(
        body,
        out_shape=out_shape,
        in_specs=specs,
        out_specs=jax.tree.map(lambda _: vmem, out_shape),
        scratch_shapes=scratch,
        compiler_params=pltpu.CompilerParams(vmem_limit_bytes=VMEM_LIMIT),
        cost_estimate=cost,
    )(*operands)


def fed_call(body, out_shape, scratch, cost, sec, fresh, *operands):
    vmem = pl.BlockSpec(memory_space=pltpu.VMEM)
    grid_spec = pltpu.PrefetchScalarGridSpec(
        num_scalar_prefetch=1,
        grid=(1,),
        in_specs=[pl.BlockSpec((1,) + fresh.shape[1:], lambda i, sec: (sec[0], 0, 0))] + [vmem] * len(operands),
        out_specs=jax.tree.map(lambda _: vmem, out_shape),
        scratch_shapes=scratch,
    )
    return pl.pallas_call(
        body,
        out_shape=out_shape,
        grid_spec=grid_spec,
        compiler_params=pltpu.CompilerParams(vmem_limit_bytes=VMEM_LIMIT),
        cost_estimate=cost,
    )(sec, fresh, *operands)


def cost(us):
    return pl.CostEstimate(flops=0, bytes_accessed=int(us * 3.0e6), transcendentals=0)


def shards(
    arriving_activations,
    fresh_images,
    saved_inputs,
    arriving_gradients,
    fresh_gradients,
    feed_order,
    forward_weight,
    forward_gain,
    forward_bias,
    backward_weight,
    backward_gain,
    backward_bias,
):
    ticks = saved_inputs.shape[0]
    d = Dims(*saved_inputs.shape[2:])
    section = lax.axis_index("section").astype(jnp.int32)
    sections = lax.axis_size("section")
    ring = [(i, (i + 1) % sections) for i in range(sections)]

    act0 = interleaved(arriving_activations, d)
    grad0 = interleaved(arriving_gradients, d)
    fresh_act = interleaved(fresh_images, d)
    fresh_grad = interleaved(fresh_gradients, d)
    saved = interleaved(saved_inputs[:, 0], d)
    vectors = [
        v[0].reshape(d.cts, LANES) for v in (forward_gain, forward_bias, backward_gain, backward_bias)
    ]
    fgain, fbias, bgain, bbias = vectors

    msg = jax.ShapeDtypeStruct((d.flat, LANES), F32)
    rows = d.n * d.pix
    wide = jax.ShapeDtypeStruct((rows, d.c), F32)
    padded = pltpu.VMEM((d.padded, LANES), F32)
    cols = pltpu.VMEM((rows, 9 * d.c), BF16)

    def prep(t):
        return call(
            functools.partial(prep_kernel, d),
            (wide, wide, jax.ShapeDtypeStruct((8, LANES), F32), jax.ShapeDtypeStruct((rows, d.c), BF16)),
            [pltpu.VMEM((d.flat, LANES), F32)],
            cost(1.5),
            saved[t],
            bgain,
            bbias,
        )

    def source(t, first_block, fresh):
        if t == 0:
            return jnp.zeros((2,), jnp.int32), first_block
        return jnp.stack([feed_order[t - 1], section]), fresh

    def backward(t, arrived, prepared):
        sec, fresh = source(t, grad0, fresh_grad)
        slope, normed, rstd, _ = prepared
        return fed_call(
            functools.partial(backward_kernel, d, t == 0),
            (msg, msg),
            [padded] * 3 + [cols],
            cost(2.0),
            sec,
            fresh,
            arrived,
            slope,
            normed,
            rstd,
            backward_weight[0],
        )

    def forward(t, arrived):
        sec, fresh = source(t, act0, fresh_act)
        return fed_call(
            functools.partial(forward_kernel, d, t == 0),
            msg,
            [padded] * 3 + [cols, pltpu.VMEM((d.flat, LANES), F32)],
            cost(2.0),
            sec,
            fresh,
            arrived,
            fgain,
            fbias,
            forward_weight[0],
        )

    nothing = jnp.zeros((8, LANES), F32)
    arrived, arrived_grad = nothing, nothing
    emitted, returned, entered, hidden = [], [], [], []
    for t in range(ticks):
        prepared = prep(t)
        hidden.append(prepared[3])
        grad_out, e = backward(t, arrived_grad, prepared)
        returned.append(grad_out)
        entered.append(e)
        if t < ticks - 1:
            arrived_grad = lax.ppermute(grad_out, "section", ring)
        act_out = forward(t, arrived)
        emitted.append(act_out)
        if t < ticks - 1:
            arrived = lax.ppermute(act_out, "section", ring)

    n = lax.axis_size("dp")
    order = list(range(0, n, 2)) + list(range(n - 1 - n % 2, 0, -2))
    place = [order.index(i) for i in range(n)]
    chunk = 9 * d.c // n
    places = jnp.array(place, jnp.int32)
    me = places[lax.axis_index("dp")]
    slots = jnp.concatenate([(me - 1 - places) % n, (places - me - 1) % n])
    factor = 1.0 / (n * d.n)
    half = jax.ShapeDtypeStruct((n, chunk, LANES), F32)
    up, down = call(
        functools.partial(weight_kernel, d, ticks, chunk, factor),
        (half, half),
        [padded] * 3 + [pltpu.VMEM((ticks * rows, 9 * d.c), BF16), pltpu.VMEM((ticks * rows, d.c), BF16)],
        cost(4.0),
        slots,
        *entered,
        *hidden,
    )
    onward = [(order[i], order[(i + 1) % n]) for i in range(n)]
    back = [(b, a) for a, b in onward]
    a, b = up[0], down[0]
    for s in range(1, n):
        a, b = lax.ppermute(a, "dp", onward), lax.ppermute(b, "dp", back)
        a, b = a + up[s], b + down[s]
    shard_sum = jnp.concatenate([a, b], axis=1)
    return (
        jnp.stack([standard(v, d) for v in emitted])[:, None],
        jnp.stack([standard(v, d) for v in returned])[:, None],
        shard_sum[None],
    )


def solution(mesh):
    placed = (
        P("section", "dp", None, None, None),
        P(None, "dp", None, None, None),
        P(None, "section", "dp", None, None, None),
        P("section", "dp", None, None, None),
        P(None, "dp", None, None, None),
        P(),
        P("section", None, None),
        P("section", None),
        P("section", None),
        P("section", None, None),
        P("section", None),
        P("section", None),
    )
    return jax.shard_map(
        shards,
        mesh=mesh,
        in_specs=placed,
        out_specs=(
            P(None, "section", "dp", None, None, None),
            P(None, "section", "dp", None, None, None),
            P("section", "dp", None),
        ),
        check_vma=False,
    )
```

```python
import functools
import math

import jax
import jax.numpy as jnp
from jax import lax
from jax.experimental import pallas as pl
from jax.experimental.pallas import tpu as pltpu
from jax.sharding import PartitionSpec as P

GROUPS = 32
F32 = jnp.float32
BF16 = jnp.bfloat16
LANES = 128
VMEM_LIMIT = 24 * 1024 * 1024


class Dims:
    def __init__(self, images, rows, cols, channels):
        self.n, self.h, self.w, self.c = images, rows, cols, channels
        self.cts = channels // LANES
        self.unit = self.cts * images
        self.pix = rows * cols
        self.flat = self.pix * self.unit
        per = 8 // math.gcd(8, self.unit)
        self.pad = -(-(cols + 1) // per) * per
        self.padded = (self.pix + 2 * self.pad) * self.unit
        self.count = self.pix * (channels // GROUPS)


def interleaved(x, d):
    lead = x.shape[:-4]
    k = len(lead)
    x = x.reshape(*lead, d.n, d.pix, d.cts, LANES)
    x = x.transpose(*range(k), k + 1, k + 2, k, k + 3)
    return x.reshape(*lead, d.flat, LANES)


def standard(x, d):
    lead = x.shape[:-2]
    k = len(lead)
    x = x.reshape(*lead, d.pix, d.cts, d.n, LANES)
    x = x.transpose(*range(k), k + 2, k, k + 1, k + 3)
    return x.reshape(*lead, d.n, d.h, d.w, d.c)


def group_sum(v, width):
    lane = lax.broadcasted_iota(jnp.int32, v.shape, 1)
    k = 1
    while k < width:
        v = v + jnp.where((lane & k) == 0, pltpu.roll(v, LANES - k, 1), pltpu.roll(v, k, 1))
        k *= 2
    return v


def pattern(ref, d):
    row = lax.broadcasted_iota(jnp.int32, (8, LANES), 0)
    ct = (row // d.n) % d.cts
    out = jnp.broadcast_to(ref[0:1, :], (8, LANES))
    for i in range(1, d.cts):
        out = jnp.where(ct == i, jnp.broadcast_to(ref[i : i + 1, :], (8, LANES)), out)
    return out


def unit_sum(v, d):
    s = jnp.sum(v, axis=0)
    k = d.unit
    while k < 8:
        s = s + pltpu.roll(s, k, 0)
        k *= 2
    return group_sum(s, d.c // GROUPS)


def normalized(x, d):
    tiles = x.reshape(-1, 8, LANES)
    scale = 1.0 / d.count
    mean = unit_sum(tiles, d) * scale
    centred = tiles - mean
    var = unit_sum(centred * centred, d) * scale
    rstd = lax.rsqrt(var + 1e-05)
    return centred * rstd, rstd


def sigmoid(a):
    return 0.5 * jnp.tanh(0.5 * a) + 0.5


def spread(value, refs, d):
    zeros = jnp.zeros((d.pad * d.unit, LANES), F32)
    for ref in refs:
        ref[0 : d.pad * d.unit, :] = zeros
        ref[d.padded - d.pad * d.unit : d.padded, :] = zeros
        ref[d.pad * d.unit : d.pad * d.unit + d.flat, :] = value
    edge = jnp.zeros((d.unit, LANES), F32)
    for i in range(d.h):
        last = (d.pad + i * d.w + d.w - 1) * d.unit
        first = (d.pad + i * d.w) * d.unit
        refs[0][last : last + d.unit, :] = edge
        refs[2][first : first + d.unit, :] = edge


def plane(ref, d, shift, n):
    parts = [
        ref[pl.ds((d.pad + shift) * d.unit + ct * d.n + n, d.pix, stride=d.unit), :] for ct in range(d.cts)
    ]
    return jnp.concatenate(parts, axis=1)


def gather_patches(refs, out_ref, d):
    for kr in range(3):
        for kc in range(3):
            tap = kr * 3 + kc
            for n in range(d.n):
                block = plane(refs[kc], d, (kr - 1) * d.w + kc - 1, n)
                out_ref[n * d.pix : (n + 1) * d.pix, tap * d.c : (tap + 1) * d.c] = block.astype(BF16)


def from_interleaved(ref, d, base=0):
    rows = [
        jnp.concatenate(
            [ref[pl.ds(base + ct * d.n + n, d.pix, stride=d.unit), :] for ct in range(d.cts)], axis=1
        )
        for n in range(d.n)
    ]
    return jnp.concatenate(rows, axis=0)


def to_interleaved(ref, n, value, d):
    for ct in range(d.cts):
        ref[pl.ds(ct * d.n + n, d.pix, stride=d.unit), :] = value[:, ct * LANES : (ct + 1) * LANES]


def prep_kernel(d, saved_ref, gain_ref, bias_ref, slope_ref, normed_ref, rstd_ref, hidden_ref, tmp):
    x = saved_ref[0].astype(F32)
    normed, rstd = normalized(x, d)
    gain = pattern(gain_ref, d)
    a = normed * gain + pattern(bias_ref, d)
    s = sigmoid(a)
    rstd_ref[...] = rstd
    for ref, value in (
        (normed_ref, normed),
        (slope_ref, s * (1.0 + a * (1.0 - s)) * gain),
        (hidden_ref, a * s),
    ):
        tmp[...] = value.reshape(d.flat, LANES)
        ref[...] = from_interleaved(tmp, d).astype(ref.dtype)


def entering(first, fresh_ref, arrived_ref):
    fresh = fresh_ref[0].astype(F32)
    if first:
        return fresh
    return jnp.where(lax.axis_index("section") == 0, fresh, arrived_ref[...])


def keep(out_ref, all_ref, tick, sem):
    copy = pltpu.make_async_copy(out_ref, all_ref.at[tick], sem)
    copy.start()
    copy.wait()


def backward_kernel(
    d,
    tick,
    feed_ref,
    fresh_ref,
    arrived_ref,
    slope_ref,
    normed_ref,
    rstd_ref,
    weight_ref,
    kept_ref,
    out_ref,
    e_ref,
    all_ref,
    left,
    mid,
    right,
    cols,
    sem,
):
    e = entering(tick == 0, fresh_ref, arrived_ref)
    e_ref[...] = e
    spread(e, (left, mid, right), d)
    gather_patches((left, mid, right), cols, d)
    grad = None
    for tap in range(9):
        part = lax.dot_general(
            cols[:, tap * d.c : (tap + 1) * d.c],
            weight_ref[(8 - tap) * d.c : (9 - tap) * d.c, :],
            (((1,), (1,)), ((), ())),
            preferred_element_type=F32,
        )
        grad = part if grad is None else grad + part
    through = grad * slope_ref[...]
    weighted = through * normed_ref[...]
    rows = []
    for ct in range(d.cts):
        for n in range(d.n):
            for v in (through, weighted):
                rows.append(
                    jnp.sum(v[n * d.pix : (n + 1) * d.pix, ct * LANES : (ct + 1) * LANES], axis=0, keepdims=True)
                )
    sums = group_sum(jnp.concatenate(rows, axis=0), d.c // GROUPS) * (1.0 / d.count)
    for n in range(d.n):
        for ct in range(d.cts):
            k = (ct * d.n + n) * 2
            here = (slice(n * d.pix, (n + 1) * d.pix), slice(ct * LANES, (ct + 1) * LANES))
            rstd = rstd_ref[ct * d.n + n : ct * d.n + n + 1, :]
            value = (through[here] - sums[k : k + 1] - normed_ref[here] * sums[k + 1 : k + 2]) * rstd
            where = ct * d.n + n
            e_here = mid[pl.ds(d.pad * d.unit + where, d.pix, stride=d.unit), :]
            out_ref[pl.ds(where, d.pix, stride=d.unit), :] = value + e_here
    keep(out_ref, all_ref, tick, sem)


def forward_kernel(
    d,
    tick,
    feed_ref,
    fresh_ref,
    arrived_ref,
    gain_ref,
    bias_ref,
    weight_ref,
    kept_ref,
    out_ref,
    all_ref,
    left,
    mid,
    right,
    cols,
    kept,
    sem,
):
    x = entering(tick == 0, fresh_ref, arrived_ref)
    kept[...] = x
    normed, _ = normalized(x, d)
    a = normed * pattern(gain_ref, d) + pattern(bias_ref, d)
    hidden = (a * sigmoid(a)).reshape(d.flat, LANES)
    spread(hidden, (left, mid, right), d)
    gather_patches((left, mid, right), cols, d)
    conv = jnp.dot(cols[...], weight_ref[...], preferred_element_type=F32)
    for n in range(d.n):
        for ct in range(d.cts):
            where = pl.ds(ct * d.n + n, d.pix, stride=d.unit)
            out_ref[where, :] = (
                kept[where, :] + conv[n * d.pix : (n + 1) * d.pix, ct * LANES : (ct + 1) * LANES]
            )
    keep(out_ref, all_ref, tick, sem)


def weight_kernel(d, ticks, n, place, factor, *refs):
    e_refs, h_refs = refs[:ticks], refs[ticks : 2 * ticks]
    streams = refs[2 * ticks : 2 * ticks + 4]
    left, mid, right, cols, hid = refs[2 * ticks + 4 :]
    me = lax.axis_index("dp")
    me = jnp.where(me % 2 == 0, me // 2, n - 1 - me // 2)
    rows = d.n * d.pix
    chunk = 9 * d.c // n
    for t in range(ticks):
        spread(e_refs[t][...], (left, mid, right), d)
        gather_patches((left, mid, right), cols.at[t * rows : (t + 1) * rows], d)
        hid[t * rows : (t + 1) * rows, :] = h_refs[t][...]
    h = hid[...]
    for tap in range(9):
        block = lax.dot_general(
            h, cols[:, (8 - tap) * d.c : (9 - tap) * d.c], (((0,), (0,)), ((), ())), preferred_element_type=F32
        ) * factor
        at = tap * d.c
        while at < (tap + 1) * d.c:
            owner = at // chunk
            part = (at % chunk) // (chunk // 2)
            start = owner * chunk + part * (chunk // 2)
            stop = min(start + chunk // 2, (tap + 1) * d.c)
            piece = block[at - tap * d.c : stop - tap * d.c]
            where = pl.ds(at - start, stop - at)
            up = (me - 1 - place[owner] + n) % n
            down = (place[owner] - me - 1 + n) % n
            streams[2 * part][up, where, :] = piece[:, :LANES]
            streams[2 * part + 1][down, where, :] = piece[:, LANES:]
            at = stop


def cost(us):
    return pl.CostEstimate(flops=0, bytes_accessed=int(us * 3.0e6), transcendentals=0)


VMEM = pl.BlockSpec(memory_space=pltpu.VMEM)
ANY = pl.BlockSpec(memory_space=pl.ANY)


def call(body, out_shape, scratch, us, *operands, in_specs=None, out_specs=None, feed=None, alias=None):
    in_specs = in_specs or [VMEM] * len(operands)
    out_specs = out_specs or jax.tree.map(lambda _: VMEM, out_shape)
    scalars = [] if feed is None else [feed]
    return pl.pallas_call(
        body,
        out_shape=out_shape,
        grid_spec=pltpu.PrefetchScalarGridSpec(
            num_scalar_prefetch=len(scalars), grid=(1,), in_specs=in_specs, out_specs=out_specs, scratch_shapes=scratch
        ),
        compiler_params=pltpu.CompilerParams(vmem_limit_bytes=VMEM_LIMIT),
        cost_estimate=cost(us),
        input_output_aliases=alias or {},
    )(*scalars, *operands)


def shards(
    arriving_activations,
    fresh_images,
    saved_inputs,
    arriving_gradients,
    fresh_gradients,
    feed_order,
    forward_weight,
    forward_gain,
    forward_bias,
    backward_weight,
    backward_gain,
    backward_bias,
):
    ticks = saved_inputs.shape[0]
    d = Dims(*saved_inputs.shape[2:])
    sections = lax.axis_size("section")
    ring = [(i, (i + 1) % sections) for i in range(sections)]

    act0 = interleaved(arriving_activations, d)
    grad0 = interleaved(arriving_gradients, d)
    fresh_act = interleaved(fresh_images, d)
    fresh_grad = interleaved(fresh_gradients, d)
    saved = interleaved(saved_inputs[:, 0], d)
    fgain, fbias, bgain, bbias = [
        v[0].reshape(d.cts, LANES) for v in (forward_gain, forward_bias, backward_gain, backward_bias)
    ]

    msg = jax.ShapeDtypeStruct((d.flat, LANES), F32)
    every = jax.ShapeDtypeStruct((ticks, d.flat, LANES), F32)
    rows = d.n * d.pix
    wide = jax.ShapeDtypeStruct((rows, d.c), F32)
    padded = pltpu.VMEM((d.padded, LANES), F32)
    cols = pltpu.VMEM((rows, 9 * d.c), BF16)
    flat = pltpu.VMEM((d.flat, LANES), F32)
    sem = pltpu.SemaphoreType.DMA

    def block(index):
        return pl.BlockSpec((1, d.flat, LANES), index)

    def prep(t):
        return call(
            functools.partial(prep_kernel, d),
            (wide, wide, jax.ShapeDtypeStruct((8, LANES), F32), jax.ShapeDtypeStruct((rows, d.c), BF16)),
            [flat],
            0.8,
            saved,
            bgain,
            bbias,
            in_specs=[block(lambda i: (t, 0, 0)), VMEM, VMEM],
        )

    def fed(t, body, outs, scratch, us, first, fresh, arrived, kept, *more):
        index = (lambda i, feed: (0, 0, 0)) if t == 0 else (lambda i, feed: (feed[t - 1], 0, 0))
        operands = [first if t == 0 else fresh, arrived, *more, kept]
        return call(
            functools.partial(body, d, t),
            (*outs, every),
            scratch,
            us,
            *operands,
            in_specs=[block(index)] + [VMEM] * (len(operands) - 2) + [ANY],
            out_specs=tuple([VMEM] * len(outs) + [ANY]),
            feed=feed_order,
            alias={} if t == 0 else {len(operands): len(outs)},
        )

    nothing = jnp.zeros((8, LANES), F32)
    arrived, arrived_grad, emitted, returned = [nothing] * 4
    entered, hidden = [], []
    for t in range(ticks):
        slope, normed, rstd, h = prep(t)
        hidden.append(h)
        grad_out, e, returned = fed(
            t,
            backward_kernel,
            (msg, msg),
            [padded] * 3 + [cols, sem],
            1.5,
            grad0,
            fresh_grad,
            arrived_grad,
            returned,
            slope,
            normed,
            rstd,
            backward_weight[0],
        )
        entered.append(e)
        if t < ticks - 1:
            arrived_grad = lax.ppermute(grad_out, "section", ring)
        act_out, emitted = fed(
            t,
            forward_kernel,
            (msg,),
            [padded] * 3 + [cols, flat, sem],
            1.7,
            act0,
            fresh_act,
            arrived,
            emitted,
            fgain,
            fbias,
            forward_weight[0],
        )
        if t < ticks - 1:
            arrived = lax.ppermute(act_out, "section", ring)

    n = lax.axis_size("dp")
    order = list(range(0, n, 2)) + list(range(n - 1 - n % 2, 0, -2))
    place = [order.index(i) for i in range(n)]
    chunk = 9 * d.c // n
    half = jax.ShapeDtypeStruct((n, chunk // 2, LANES), F32)
    streams = call(
        functools.partial(weight_kernel, d, ticks, n, place, 1.0 / (n * d.n)),
        (half,) * 4,
        [padded] * 3 + [pltpu.VMEM((ticks * rows, 9 * d.c), BF16), pltpu.VMEM((ticks * rows, d.c), BF16)],
        2.7,
        *entered,
        *hidden,
    )
    onward = [(order[i], order[(i + 1) % n]) for i in range(n)]
    back = [(b, a) for a, b in onward]
    sums = [v[0] for v in streams]
    for s in range(1, n):
        for i in range(4):
            sums[i] = lax.ppermute(sums[i], "dp", back if i % 2 else onward) + streams[i][s]
    shard_sum = jnp.concatenate(
        [jnp.concatenate(sums[:2], axis=1), jnp.concatenate(sums[2:], axis=1)], axis=0
    )
    return standard(emitted, d)[:, None], standard(returned, d)[:, None], shard_sum[None]


def solution(mesh):
    placed = (
        P("section", "dp", None, None, None),
        P(None, "dp", None, None, None),
        P(None, "section", "dp", None, None, None),
        P("section", "dp", None, None, None),
        P(None, "dp", None, None, None),
        P(),
        P("section", None, None),
        P("section", None),
        P("section", None),
        P("section", None, None),
        P("section", None),
        P("section", None),
    )
    return jax.shard_map(
        shards,
        mesh=mesh,
        in_specs=placed,
        out_specs=(
            P(None, "section", "dp", None, None, None),
            P(None, "section", "dp", None, None, None),
            P("section", "dp", None),
        ),
        check_vma=False,
    )
```

```python
import functools
import math

import jax
import jax.numpy as jnp
from jax import lax
from jax.experimental import pallas as pl
from jax.experimental.pallas import tpu as pltpu
from jax.sharding import PartitionSpec as P

GROUPS = 32
F32 = jnp.float32
BF16 = jnp.bfloat16
LANES = 128
VMEM_LIMIT = 24 * 1024 * 1024
WHOLE_VMEM = 60 * 1024 * 1024


class Dims:
    def __init__(self, images, rows, cols, channels):
        self.n, self.h, self.w, self.c = images, rows, cols, channels
        self.cts = channels // LANES
        self.unit = self.cts * images
        self.pix = rows * cols
        self.flat = self.pix * self.unit
        per = 8 // math.gcd(8, self.unit)
        self.pad = -(-(cols + 1) // per) * per
        self.padded = (self.pix + 2 * self.pad) * self.unit
        self.count = self.pix * (channels // GROUPS)


def interleaved(x, d):
    lead = x.shape[:-4]
    k = len(lead)
    x = x.reshape(*lead, d.n, d.pix, d.cts, LANES)
    x = x.transpose(*range(k), k + 1, k + 2, k, k + 3)
    return x.reshape(*lead, d.flat, LANES)


def standard(x, d):
    lead = x.shape[:-2]
    k = len(lead)
    x = x.reshape(*lead, d.pix, d.cts, d.n, LANES)
    x = x.transpose(*range(k), k + 2, k, k + 1, k + 3)
    return x.reshape(*lead, d.n, d.h, d.w, d.c)


def group_sum(v, width):
    lane = lax.broadcasted_iota(jnp.int32, v.shape, 1)
    k = 1
    while k < width:
        v = v + jnp.where((lane & k) == 0, pltpu.roll(v, LANES - k, 1), pltpu.roll(v, k, 1))
        k *= 2
    return v


def pattern(ref, d):
    row = lax.broadcasted_iota(jnp.int32, (8, LANES), 0)
    ct = (row // d.n) % d.cts
    out = jnp.broadcast_to(ref[0:1, :], (8, LANES))
    for i in range(1, d.cts):
        out = jnp.where(ct == i, jnp.broadcast_to(ref[i : i + 1, :], (8, LANES)), out)
    return out


def unit_sum(v, d):
    s = jnp.sum(v, axis=0)
    k = d.unit
    while k < 8:
        s = s + pltpu.roll(s, k, 0)
        k *= 2
    return group_sum(s, d.c // GROUPS)


def normalized(x, d):
    tiles = x.reshape(-1, 8, LANES)
    scale = 1.0 / d.count
    mean = unit_sum(tiles, d) * scale
    centred = tiles - mean
    var = unit_sum(centred * centred, d) * scale
    rstd = lax.rsqrt(var + 1e-05)
    return centred * rstd, rstd


def sigmoid(a):
    return 0.5 * jnp.tanh(0.5 * a) + 0.5


def spread(value, refs, d):
    zeros = jnp.zeros((d.pad * d.unit, LANES), F32)
    for ref in refs:
        ref[0 : d.pad * d.unit, :] = zeros
        ref[d.padded - d.pad * d.unit : d.padded, :] = zeros
        ref[d.pad * d.unit : d.pad * d.unit + d.flat, :] = value
    edge = jnp.zeros((d.unit, LANES), F32)
    for i in range(d.h):
        last = (d.pad + i * d.w + d.w - 1) * d.unit
        first = (d.pad + i * d.w) * d.unit
        refs[0][last : last + d.unit, :] = edge
        refs[2][first : first + d.unit, :] = edge


def plane(ref, d, shift, n):
    parts = [
        ref[pl.ds((d.pad + shift) * d.unit + ct * d.n + n, d.pix, stride=d.unit), :] for ct in range(d.cts)
    ]
    return jnp.concatenate(parts, axis=1)


def gather_patches(refs, out_ref, d):
    for kr in range(3):
        for kc in range(3):
            tap = kr * 3 + kc
            for n in range(d.n):
                block = plane(refs[kc], d, (kr - 1) * d.w + kc - 1, n)
                out_ref[n * d.pix : (n + 1) * d.pix, tap * d.c : (tap + 1) * d.c] = block.astype(BF16)


def from_interleaved(ref, d, base=0):
    rows = [
        jnp.concatenate(
            [ref[pl.ds(base + ct * d.n + n, d.pix, stride=d.unit), :] for ct in range(d.cts)], axis=1
        )
        for n in range(d.n)
    ]
    return jnp.concatenate(rows, axis=0)


def to_interleaved(ref, n, value, d):
    for ct in range(d.cts):
        ref[pl.ds(ct * d.n + n, d.pix, stride=d.unit), :] = value[:, ct * LANES : (ct + 1) * LANES]


def prepare(d, x, gain_ref, bias_ref, slope_ref, normed_ref, hidden_ref, tmp):
    normed, rstd = normalized(x, d)
    gain = pattern(gain_ref, d)
    a = normed * gain + pattern(bias_ref, d)
    s = sigmoid(a)
    for ref, value in (
        (normed_ref, normed),
        (slope_ref, s * (1.0 + a * (1.0 - s)) * gain),
        (hidden_ref, a * s),
    ):
        tmp[...] = value.reshape(d.flat, LANES)
        ref[...] = from_interleaved(tmp, d).astype(ref.dtype)
    return rstd


def prep_kernel(d, saved_ref, gain_ref, bias_ref, after_ref, slope_ref, normed_ref, rstd_ref, hidden_ref, tmp):
    for k in range(slope_ref.shape[0]):
        x = saved_ref[k + 1].astype(F32)
        refs = [r.at[k] for r in (slope_ref, normed_ref, hidden_ref)]
        rstd_ref[k] = prepare(d, x, gain_ref, bias_ref, *refs, tmp)


def through_layer(d, cols, weight_ref, slope_ref, normed_ref, rstd_at, mid, out_ref):
    grad = None
    for tap in range(9):
        part = lax.dot_general(
            cols[:, tap * d.c : (tap + 1) * d.c],
            weight_ref[(8 - tap) * d.c : (9 - tap) * d.c, :],
            (((1,), (1,)), ((), ())),
            preferred_element_type=F32,
        )
        grad = part if grad is None else grad + part
    through = grad * slope_ref[...]
    weighted = through * normed_ref[...]
    rows = []
    for ct in range(d.cts):
        for n in range(d.n):
            for v in (through, weighted):
                rows.append(
                    jnp.sum(v[n * d.pix : (n + 1) * d.pix, ct * LANES : (ct + 1) * LANES], axis=0, keepdims=True)
                )
    sums = group_sum(jnp.concatenate(rows, axis=0), d.c // GROUPS) * (1.0 / d.count)
    for n in range(d.n):
        for ct in range(d.cts):
            where = ct * d.n + n
            k = where * 2
            here = (slice(n * d.pix, (n + 1) * d.pix), slice(ct * LANES, (ct + 1) * LANES))
            value = (through[here] - sums[k : k + 1] - normed_ref[here] * sums[k + 1 : k + 2]) * rstd_at(where)
            e_here = mid[pl.ds(d.pad * d.unit + where, d.pix, stride=d.unit), :]
            out_ref[pl.ds(where, d.pix, stride=d.unit), :] = value + e_here


def first_kernel(d, feed_ref, saved_hbm, grad_hbm, gain_hbm, bias_hbm, weight_hbm, fresh_act_hbm, fresh_grad_hbm, *refs):
    out_ref, e_ref, hidden_ref, acts_ref, grads_ref = refs[:5]
    saved, grad, gain, bias, weight, slope, normed, tmp, left, mid, right, cols, sems = refs[5:]
    pairs = [(grad_hbm.at[0], grad), (saved_hbm.at[0], saved), (gain_hbm, gain), (bias_hbm, bias), (weight_hbm, weight)]
    for src, dst in ((fresh_act_hbm, acts_ref), (fresh_grad_hbm, grads_ref)):
        for k in range(feed_ref.shape[0]):
            pairs.append((src.at[feed_ref[k]], dst.at[k]))
    copies = [pltpu.make_async_copy(src, dst, sems.at[i]) for i, (src, dst) in enumerate(pairs)]
    for copy in copies:
        copy.start()
    copies[0].wait()
    e = grad[...].astype(F32)
    e_ref[...] = e
    spread(e, (left, mid, right), d)
    gather_patches((left, mid, right), cols, d)
    for copy in copies[1:4]:
        copy.wait()
    rstd = prepare(d, saved[...].astype(F32), gain, bias, slope, normed, hidden_ref, tmp)
    copies[4].wait()
    through_layer(d, cols, weight, slope, normed, lambda i: rstd[i : i + 1, :], mid, out_ref)
    for copy in copies[5:]:
        copy.wait()


def backward_kernel(
    d, tick, grads_ref, arrived_ref, slope_ref, normed_ref, rstd_ref, weight_ref, after_ref, out_ref, e_ref, left, mid, right, cols
):
    k = tick - 1
    e = jnp.where(lax.axis_index("section") == 0, grads_ref[k].astype(F32), arrived_ref[...])
    e_ref[...] = e
    spread(e, (left, mid, right), d)
    gather_patches((left, mid, right), cols, d)
    through_layer(
        d, cols, weight_ref, slope_ref.at[k], normed_ref.at[k], lambda i: rstd_ref[k, i : i + 1, :], mid, out_ref
    )


def forward_kernel(d, tick, last, fresh_ref, arrived_ref, grad_ref, act_ref, gain_ref, bias_ref, weight_ref, *refs):
    out_ref, emitted_ref, returned_ref, left, mid, right, cols, kept, sems = refs[3:]
    stores = [pltpu.make_async_copy(grad_ref, returned_ref.at[tick], sems.at[0])]
    if tick > 0:
        stores.append(pltpu.make_async_copy(act_ref, emitted_ref.at[tick - 1], sems.at[1]))
    for store in stores:
        store.start()
    x = fresh_ref[max(tick - 1, 0)].astype(F32)
    if tick > 0:
        x = jnp.where(lax.axis_index("section") == 0, x, arrived_ref[...])
    kept[...] = x
    normed, _ = normalized(x, d)
    a = normed * pattern(gain_ref, d) + pattern(bias_ref, d)
    hidden = (a * sigmoid(a)).reshape(d.flat, LANES)
    spread(hidden, (left, mid, right), d)
    gather_patches((left, mid, right), cols, d)
    conv = jnp.dot(cols[...], weight_ref[...], preferred_element_type=F32)
    for n in range(d.n):
        for ct in range(d.cts):
            where = pl.ds(ct * d.n + n, d.pix, stride=d.unit)
            out_ref[where, :] = (
                kept[where, :] + conv[n * d.pix : (n + 1) * d.pix, ct * LANES : (ct + 1) * LANES]
            )
    if last:
        stores.append(pltpu.make_async_copy(out_ref, emitted_ref.at[tick], sems.at[2]))
        stores[-1].start()
    for store in stores:
        store.wait()


def slot(owner, me, order):
    differ = jnp.bitwise_xor(me, owner)
    out = 0
    for bit in order:
        out = out * 2 + jnp.bitwise_and(lax.shift_right_logical(differ, bit), 1)
    return out


def weight_kernel(d, ticks, n, orders, factor, *refs):
    added = ticks == 0
    if added:
        grads_ref, arrived_ref, hid = refs[0], refs[1], refs[2].at[refs[2].shape[0] - 1]
        before, streams = refs[3:7], refs[7:11]
        left, mid, right, cols = refs[11:]
        section = lax.axis_index("section")
        entered = [jnp.where(section == 0, grads_ref[grads_ref.shape[0] - 1].astype(F32), arrived_ref[...])]
    else:
        entered = [ref[...] for ref in refs[:ticks]]
        streams = refs[ticks + 2 : ticks + 6]
        left, mid, right, cols, hid = refs[ticks + 6 :]
    me = lax.axis_index("dp")
    rows = d.n * d.pix
    chunk = 9 * d.c // n
    for t, e in enumerate(entered):
        spread(e, (left, mid, right), d)
        gather_patches((left, mid, right), cols.at[t * rows : (t + 1) * rows], d)
        if not added:
            hid[t * rows : (t + 1) * rows, :] = refs[ticks][...] if t == 0 else refs[ticks + 1][t - 1]
    h = hid[...]
    for tap in range(9):
        block = lax.dot_general(
            h, cols[:, (8 - tap) * d.c : (9 - tap) * d.c], (((0,), (0,)), ((), ())), preferred_element_type=F32
        ) * factor
        at = tap * d.c
        while at < (tap + 1) * d.c:
            owner = at // chunk
            part = (at % chunk) // (chunk // 2)
            start = owner * chunk + part * (chunk // 2)
            stop = min(start + chunk // 2, (tap + 1) * d.c)
            where = pl.ds(at - start, stop - at)
            slots = [slot(owner, me, order) for order in orders]
            for way in range(2):
                piece = block[at - tap * d.c : stop - tap * d.c, way * LANES : (way + 1) * LANES]
                if added:
                    piece = piece + before[2 * part + way][slots[way], where, :]
                streams[2 * part + way][slots[way], where, :] = piece
            at = stop


def cost(us):
    return pl.CostEstimate(flops=0, bytes_accessed=int(us * 3.0e6), transcendentals=0)


VMEM = pl.BlockSpec(memory_space=pltpu.VMEM)
HBM = pl.BlockSpec(memory_space=pltpu.HBM)
SMEM = pl.BlockSpec(memory_space=pltpu.SMEM)
ANY = pl.BlockSpec(memory_space=pl.ANY)


def call(body, out_shape, scratch, us, *operands, in_specs=None, out_specs=None, alias=None, vmem=VMEM_LIMIT):
    return pl.pallas_call(
        body,
        out_shape=out_shape,
        in_specs=in_specs or [VMEM] * len(operands),
        out_specs=out_specs or jax.tree.map(lambda _: VMEM, out_shape),
        scratch_shapes=scratch,
        compiler_params=pltpu.CompilerParams(vmem_limit_bytes=vmem),
        cost_estimate=cost(us),
        input_output_aliases=alias or {},
    )(*operands)


def shards(
    arriving_activations,
    fresh_images,
    saved_inputs,
    arriving_gradients,
    fresh_gradients,
    feed_order,
    forward_weight,
    forward_gain,
    forward_bias,
    backward_weight,
    backward_gain,
    backward_bias,
):
    ticks = saved_inputs.shape[0]
    d = Dims(*saved_inputs.shape[2:])
    sections = lax.axis_size("section")
    ring = [(i, (i + 1) % sections) for i in range(sections)]

    act0 = interleaved(arriving_activations, d)
    grad0 = interleaved(arriving_gradients, d)
    fresh_act = interleaved(fresh_images, d)
    fresh_grad = interleaved(fresh_gradients, d)
    saved = interleaved(saved_inputs[:, 0], d)
    fgain, fbias, bgain, bbias = [
        v[0].reshape(d.cts, LANES) for v in (forward_gain, forward_bias, backward_gain, backward_bias)
    ]

    msg = jax.ShapeDtypeStruct((d.flat, LANES), F32)
    every = jax.ShapeDtypeStruct((ticks, d.flat, LANES), F32)
    rows = d.n * d.pix
    wide = jax.ShapeDtypeStruct((rows, d.c), F32)
    padded = pltpu.VMEM((d.padded, LANES), F32)
    cols = pltpu.VMEM((rows, 9 * d.c), BF16)
    flat = pltpu.VMEM((d.flat, LANES), F32)
    sem = pltpu.SemaphoreType.DMA

    whole = pltpu.VMEM((rows, d.c), F32)
    vector = pltpu.VMEM((d.cts, LANES), F32)
    narrow = jax.ShapeDtypeStruct((rows, d.c), BF16)
    raw = pltpu.VMEM((d.flat, LANES), BF16)

    last = ticks - 1

    def later(shape, dtype):
        return jax.ShapeDtypeStruct((last, *shape), dtype)

    def first():
        entering = later((d.flat, LANES), BF16)
        return call(
            functools.partial(first_kernel, d),
            (msg, msg, narrow, entering, entering),
            [raw, raw, vector, vector, pltpu.VMEM(backward_weight.shape[1:], BF16), whole, whole, flat]
            + [padded] * 3
            + [cols, sem((5 + 2 * last,))],
            2.5,
            feed_order,
            saved,
            grad0,
            bgain,
            bbias,
            backward_weight[0],
            fresh_act,
            fresh_grad,
            in_specs=[SMEM] + [HBM] * 7,
            vmem=WHOLE_VMEM,
        )

    def prep(after):
        return call(
            functools.partial(prep_kernel, d),
            (later((rows, d.c), F32), later((rows, d.c), F32), later((8, LANES), F32), later((rows, d.c), BF16)),
            [flat],
            0.7 * last,
            saved,
            bgain,
            bbias,
            after,
            in_specs=[VMEM] * 3 + [ANY],
        )

    def backward(t, arrived, after):
        slope, normed, rstd, _ = prepared
        return call(
            functools.partial(backward_kernel, d, t),
            (msg, msg),
            [padded] * 3 + [cols],
            0.9,
            grads,
            arrived,
            slope,
            normed,
            rstd,
            backward_weight[0],
            after,
            in_specs=[VMEM] * 6 + [ANY],
        )

    def forward(t, arrived, grad_out, act_out, after, emitted, returned):
        return call(
            functools.partial(forward_kernel, d, t, t == last),
            (msg, every, every),
            [padded] * 3 + [cols, flat, sem((3,))],
            1.3,
            acts if t else act0,
            arrived,
            grad_out,
            act_out,
            fgain,
            fbias,
            forward_weight[0],
            after,
            emitted,
            returned,
            in_specs=[VMEM] * 7 + [ANY] * 3,
            out_specs=(VMEM, ANY, ANY),
            alias={8: 1, 9: 2} if t else {},
        )

    n = lax.axis_size("dp")
    bits = n.bit_length() - 1
    orders = (tuple(range(bits)), (1, 0, *range(2, bits)))
    chunk = 9 * d.c // n
    half = jax.ShapeDtypeStruct((n, chunk // 2, LANES), F32)

    def weight_terms(ticks, *operands):
        count = max(ticks, 1)
        return call(
            functools.partial(weight_kernel, d, ticks, n, orders, 1.0 / (n * d.n)),
            (half,) * 4,
            [padded] * 3
            + [pltpu.VMEM((count * rows, 9 * d.c), BF16)]
            + ([pltpu.VMEM((ticks * rows, d.c), BF16)] if ticks else []),
            0.6 * count,
            *operands,
            alias={} if ticks else {3 + i: i for i in range(4)},
        )

    nothing = jnp.zeros((8, LANES), F32)
    grad_out, e, h, acts, grads = first()
    arrived, act_out, emitted, returned = [nothing] * 4
    entered = [e]
    prepared = prep(grad_out)
    for t in range(last):
        if t > 0:
            grad_out, e = backward(t, arrived_grad, nothing)
            entered.append(e)
        arrived_grad = lax.ppermute(grad_out, "section", ring)
        after = prepared[2] if t == 0 else nothing
        act_out, emitted, returned = forward(t, arrived, grad_out, act_out, after, emitted, returned)
        arrived = lax.ppermute(act_out, "section", ring)
    before = weight_terms(last, *entered, h, prepared[3])
    streams = weight_terms(0, grads, arrived_grad, prepared[3], *before)

    def exchange(held, bit):
        half = held.shape[0] // 2
        return held[:half] + lax.ppermute(held[half:], "dp", [(i, i ^ (1 << bit)) for i in range(n)])

    done = []
    for part in range(2):
        held = [streams[2 * part], streams[2 * part + 1]]
        for i in range(2):
            held = [exchange(v, order[i]) for v, order in zip(held, orders)]
        both = jnp.concatenate(held, axis=2)
        for bit in range(2, bits):
            both = exchange(both, bit)
        done.append(both[0])
        if part == 0:
            grad_out, _ = backward(last, arrived_grad, held[0])
            act_out, emitted, returned = forward(last, arrived, grad_out, act_out, nothing, emitted, returned)
    shard_sum = jnp.concatenate(done, axis=0)
    return standard(emitted, d)[:, None], standard(returned, d)[:, None], shard_sum[None]


def solution(mesh):
    placed = (
        P("section", "dp", None, None, None),
        P(None, "dp", None, None, None),
        P(None, "section", "dp", None, None, None),
        P("section", "dp", None, None, None),
        P(None, "dp", None, None, None),
        P(),
        P("section", None, None),
        P("section", None),
        P("section", None),
        P("section", None, None),
        P("section", None),
        P("section", None),
    )
    return jax.shard_map(
        shards,
        mesh=mesh,
        in_specs=placed,
        out_specs=(
            P(None, "section", "dp", None, None, None),
            P(None, "section", "dp", None, None, None),
            P("section", "dp", None),
        ),
        check_vma=False,
    )
```

```python
import functools
import math

import jax
import jax.numpy as jnp
from jax import lax
from jax.experimental import pallas as pl
from jax.experimental.pallas import tpu as pltpu
from jax.sharding import PartitionSpec as P

GROUPS = 32
F32 = jnp.float32
BF16 = jnp.bfloat16
LANES = 128
VMEM_LIMIT = 24 * 1024 * 1024
WHOLE_VMEM = 60 * 1024 * 1024


class Dims:
    def __init__(self, images, rows, cols, channels):
        self.n, self.h, self.w, self.c = images, rows, cols, channels
        self.cts = channels // LANES
        self.unit = self.cts * images
        self.pix = rows * cols
        self.flat = self.pix * self.unit
        per = 8 // math.gcd(8, self.unit)
        self.pad = -(-(cols + 1) // per) * per
        self.padded = (self.pix + 2 * self.pad) * self.unit
        self.count = self.pix * (channels // GROUPS)


def interleaved(x, d):
    lead = x.shape[:-4]
    k = len(lead)
    x = x.reshape(*lead, d.n, d.pix, d.cts, LANES)
    x = x.transpose(*range(k), k + 1, k + 2, k, k + 3)
    return x.reshape(*lead, d.flat, LANES)


def standard(x, d):
    lead = x.shape[:-2]
    k = len(lead)
    x = x.reshape(*lead, d.pix, d.cts, d.n, LANES)
    x = x.transpose(*range(k), k + 2, k, k + 1, k + 3)
    return x.reshape(*lead, d.n, d.h, d.w, d.c)


def group_sum(v, width):
    lane = lax.broadcasted_iota(jnp.int32, v.shape, 1)
    k = 1
    while k < width:
        v = v + jnp.where((lane & k) == 0, pltpu.roll(v, LANES - k, 1), pltpu.roll(v, k, 1))
        k *= 2
    return v


def pattern(ref, d):
    row = lax.broadcasted_iota(jnp.int32, (8, LANES), 0)
    ct = (row // d.n) % d.cts
    out = jnp.broadcast_to(ref[0:1, :], (8, LANES))
    for i in range(1, d.cts):
        out = jnp.where(ct == i, jnp.broadcast_to(ref[i : i + 1, :], (8, LANES)), out)
    return out


def unit_sum(v, d):
    s = jnp.sum(v, axis=0)
    k = d.unit
    while k < 8:
        s = s + pltpu.roll(s, k, 0)
        k *= 2
    return group_sum(s, d.c // GROUPS)


def normalized(x, d):
    tiles = x.reshape(-1, 8, LANES)
    scale = 1.0 / d.count
    mean = unit_sum(tiles, d) * scale
    centred = tiles - mean
    var = unit_sum(centred * centred, d) * scale
    rstd = lax.rsqrt(var + 1e-05)
    return centred * rstd, rstd


def sigmoid(a):
    return 0.5 * jnp.tanh(0.5 * a) + 0.5


def spread(value, refs, d):
    zeros = jnp.zeros((d.pad * d.unit, LANES), F32)
    for ref in refs:
        ref[0 : d.pad * d.unit, :] = zeros
        ref[d.padded - d.pad * d.unit : d.padded, :] = zeros
        ref[d.pad * d.unit : d.pad * d.unit + d.flat, :] = value
    edge = jnp.zeros((d.unit, LANES), F32)
    for i in range(d.h):
        last = (d.pad + i * d.w + d.w - 1) * d.unit
        first = (d.pad + i * d.w) * d.unit
        refs[0][last : last + d.unit, :] = edge
        refs[2][first : first + d.unit, :] = edge


def plane(ref, d, shift, n):
    parts = [
        ref[pl.ds((d.pad + shift) * d.unit + ct * d.n + n, d.pix, stride=d.unit), :] for ct in range(d.cts)
    ]
    return jnp.concatenate(parts, axis=1)


def gather_patches(refs, out_ref, d):
    for kr in range(3):
        for kc in range(3):
            tap = kr * 3 + kc
            for n in range(d.n):
                block = plane(refs[kc], d, (kr - 1) * d.w + kc - 1, n)
                out_ref[n * d.pix : (n + 1) * d.pix, tap * d.c : (tap + 1) * d.c] = block.astype(BF16)


def from_interleaved(ref, d, base=0):
    rows = [
        jnp.concatenate(
            [ref[pl.ds(base + ct * d.n + n, d.pix, stride=d.unit), :] for ct in range(d.cts)], axis=1
        )
        for n in range(d.n)
    ]
    return jnp.concatenate(rows, axis=0)


def to_interleaved(ref, n, value, d):
    for ct in range(d.cts):
        ref[pl.ds(ct * d.n + n, d.pix, stride=d.unit), :] = value[:, ct * LANES : (ct + 1) * LANES]


def prepare(d, x, gain_ref, bias_ref, slope_ref, normed_ref, hidden_ref, tmp):
    normed, rstd = normalized(x, d)
    gain = pattern(gain_ref, d)
    a = normed * gain + pattern(bias_ref, d)
    s = sigmoid(a)
    for ref, value in (
        (normed_ref, normed),
        (slope_ref, s * (1.0 + a * (1.0 - s)) * gain),
        (hidden_ref, a * s),
    ):
        tmp[...] = value.reshape(d.flat, LANES)
        ref[...] = from_interleaved(tmp, d).astype(ref.dtype)
    return rstd


def prep_kernel(d, feed_ref, saved_ref, gain_ref, bias_ref, fresh_act_ref, fresh_grad_ref, *refs):
    slope_ref, normed_ref, rstd_ref, hidden_ref, acts_ref, grads_ref, tmp = refs
    for k in range(feed_ref.shape[0]):
        acts_ref[k] = fresh_act_ref[feed_ref[k]]
        grads_ref[k] = fresh_grad_ref[feed_ref[k]]
    for t in range(saved_ref.shape[0]):
        refs = [r.at[t] for r in (slope_ref, normed_ref, hidden_ref)]
        rstd_ref[t] = prepare(d, saved_ref[t].astype(F32), gain_ref, bias_ref, *refs, tmp)


def through_layer(d, cols, weight_ref, slope_ref, normed_ref, rstd, mid, out_ref):
    grad = None
    for tap in range(9):
        part = lax.dot_general(
            cols[:, tap * d.c : (tap + 1) * d.c],
            weight_ref[(8 - tap) * d.c : (9 - tap) * d.c, :],
            (((1,), (1,)), ((), ())),
            preferred_element_type=F32,
        )
        grad = part if grad is None else grad + part
    through = grad * slope_ref[...]
    weighted = through * normed_ref[...]
    rows = []
    for ct in range(d.cts):
        for n in range(d.n):
            for v in (through, weighted):
                rows.append(
                    jnp.sum(v[n * d.pix : (n + 1) * d.pix, ct * LANES : (ct + 1) * LANES], axis=0, keepdims=True)
                )
    sums = group_sum(jnp.concatenate(rows, axis=0), d.c // GROUPS) * (1.0 / d.count)
    for n in range(d.n):
        for ct in range(d.cts):
            where = ct * d.n + n
            k = where * 2
            here = (slice(n * d.pix, (n + 1) * d.pix), slice(ct * LANES, (ct + 1) * LANES))
            value = (through[here] - sums[k : k + 1] - normed_ref[here] * sums[k + 1 : k + 2]) * rstd[where : where + 1, :]
            e_here = mid[pl.ds(d.pad * d.unit + where, d.pix, stride=d.unit), :]
            out_ref[pl.ds(where, d.pix, stride=d.unit), :] = value + e_here


def first_kernel(d, saved_hbm, grad_hbm, gain_hbm, bias_hbm, weight_hbm, *refs):
    out_ref, saved, grad, gain, bias, weight, slope, normed, hidden, tmp, left, mid, right, cols, sems = refs

    @pl.when(chip() == 0)
    def _():
        pairs = [(grad_hbm.at[0], grad), (saved_hbm.at[0], saved), (gain_hbm, gain), (bias_hbm, bias), (weight_hbm, weight)]
        copies = [pltpu.make_async_copy(src, dst, sems.at[i]) for i, (src, dst) in enumerate(pairs)]
        for copy in copies:
            copy.start()
        copies[0].wait()
        spread(grad[...].astype(F32), (left, mid, right), d)
        gather_patches((left, mid, right), cols, d)
        for copy in copies[1:4]:
            copy.wait()
        rstd = prepare(d, saved[...].astype(F32), gain, bias, slope, normed, hidden, tmp)
        copies[4].wait()
        through_layer(d, cols, weight, slope, normed, rstd, mid, out_ref)

    @pl.when(chip() != 0)
    def _():
        out_ref[...] = jnp.zeros_like(out_ref)


def chip():
    return lax.axis_index("section") // 2


def enter(slot, grad0_ref, grads_ref, inner_ref, outer_ref, e_ref):
    tick = slot - chip()
    second = lax.axis_index("section") % 2 == 1

    @pl.when(tick == 0)
    def _():
        e_ref[...] = grad0_ref[0].astype(F32)

    @pl.when(jnp.logical_and(tick > 0, second))
    def _():
        e_ref[...] = inner_ref[...]

    @pl.when(jnp.logical_and(tick > 0, jnp.logical_and(jnp.logical_not(second), chip() > 0)))
    def _():
        e_ref[...] = outer_ref[...]

    @pl.when(jnp.logical_and(tick > 0, lax.axis_index("section") == 0))
    def _():
        e_ref[...] = grads_ref[jnp.minimum(jnp.maximum(tick - 1, 0), grads_ref.shape[0] - 1)].astype(F32)


def backward_kernel(
    d,
    slot,
    grad0_ref,
    grads_ref,
    inner_ref,
    outer_ref,
    slope_ref,
    normed_ref,
    rstd_ref,
    weight_ref,
    *refs,
):
    out_ref, e_ref, left, mid, right, cols = refs[-6:]
    tick = slot - chip()
    ticks = slope_ref.shape[0]
    runs = jnp.logical_and(tick >= 0, tick < ticks)

    @pl.when(runs)
    def _():
        t = jnp.minimum(jnp.maximum(tick, 0), ticks - 1)
        enter(slot, grad0_ref, grads_ref, inner_ref, outer_ref, e_ref)
        spread(e_ref[...], (left, mid, right), d)
        gather_patches((left, mid, right), cols, d)
        through_layer(d, cols, weight_ref, slope_ref.at[t], normed_ref.at[t], rstd_ref[t], mid, out_ref)

    @pl.when(jnp.logical_not(runs))
    def _():
        out_ref[...] = jnp.zeros_like(out_ref)
        e_ref[...] = jnp.zeros_like(e_ref)


def forward_kernel(d, tick, chips, grads, fresh_ref, arrived_ref, gain_ref, bias_ref, weight_ref, *refs):
    stores = []
    if grads:
        act_refs, grad_refs, refs = refs[:tick], refs[tick : tick + grads], refs[tick + grads :]
        out_ref, emitted_ref, returned_ref, left, mid, right, cols, kept, sems = refs
        for t in range(tick):
            stores.append(pltpu.make_async_copy(act_refs[t], emitted_ref.at[t], sems.at[t]))
            stores[-1].start()
        for t in range(tick + 1):
            for c in range(chips):

                @pl.when(chip() == c)
                def _():
                    pltpu.make_async_copy(grad_refs[t + c], returned_ref.at[t], sems.at[tick + 1 + t]).start()

            stores.append(pltpu.make_async_copy(grad_refs[t], returned_ref.at[t], sems.at[tick + 1 + t]))
    else:
        out_ref, left, mid, right, cols, kept = refs
    x = fresh_ref[max(tick - 1, 0)].astype(F32)
    if tick > 0:
        x = jnp.where(lax.axis_index("section") == 0, x, arrived_ref[...])
    kept[...] = x
    normed, _ = normalized(x, d)
    a = normed * pattern(gain_ref, d) + pattern(bias_ref, d)
    hidden = (a * sigmoid(a)).reshape(d.flat, LANES)
    spread(hidden, (left, mid, right), d)
    gather_patches((left, mid, right), cols, d)
    conv = jnp.dot(cols[...], weight_ref[...], preferred_element_type=F32)
    for n in range(d.n):
        for ct in range(d.cts):
            where = pl.ds(ct * d.n + n, d.pix, stride=d.unit)
            out_ref[where, :] = (
                kept[where, :] + conv[n * d.pix : (n + 1) * d.pix, ct * LANES : (ct + 1) * LANES]
            )
    if grads:
        stores.append(pltpu.make_async_copy(out_ref, emitted_ref.at[tick], sems.at[tick]))
        stores[-1].start()
    for store in stores:
        store.wait()


def weight_kernel(d, ticks, chips, n, positions, factor, grad0_ref, hidden_ref, *refs):
    me = lax.axis_index("dp")
    here = jnp.where(me % 2 == 0, me // 2, n - 1 - me // 2)
    rows = d.n * d.pix
    chunk = 9 * d.c // n
    last = hidden_ref.shape[0] - 1
    added = ticks == 0
    if added:
        grads_ref, inner_ref, outer_ref = refs[:3]
        e_refs, refs = refs[3 : 2 + chips], refs[2 + chips :]
        before, halves = refs[:2], refs[2:4]
        kept, left, mid, right, cols = refs[4:]
        h = hidden_ref[last]
        for c in range(chips - 1):

            @pl.when(chip() == c)
            def _():
                kept[...] = e_refs[c][...]

        @pl.when(chip() == chips - 1)
        def _():
            enter(last + chips - 1, grad0_ref, grads_ref, inner_ref, outer_ref, kept)

        spread(kept[...], (left, mid, right), d)
        gather_patches((left, mid, right), cols, d)
    else:
        e_refs, halves = refs[: ticks + chips - 2], refs[ticks + chips - 2 : ticks + chips]
        kept, left, mid, right, cols = refs[ticks + chips :]
        h = hidden_ref[0:ticks].reshape(ticks * rows, d.c)
        for t in range(ticks):
            if t == 0:
                kept[...] = grad0_ref[0].astype(F32)
            else:
                for c in range(chips):

                    @pl.when(chip() == c)
                    def _():
                        kept[...] = e_refs[t + c - 1][...]

            spread(kept[...], (left, mid, right), d)
            gather_patches((left, mid, right), cols.at[t * rows : (t + 1) * rows], d)
    for tap in range(9):
        block = lax.dot_general(
            h, cols[:, (8 - tap) * d.c : (9 - tap) * d.c], (((0,), (0,)), ((), ())), preferred_element_type=F32
        ) * factor
        at = tap * d.c
        while at < (tap + 1) * d.c:
            owner = at // chunk
            stop = min((owner + 1) * chunk, (tap + 1) * d.c)
            where = pl.ds(at - owner * chunk, stop - at)
            away = (positions[owner] - here + n) % n
            for i in range(2):
                piece = block[at - tap * d.c : stop - tap * d.c, i * LANES : (i + 1) * LANES]
                if added:
                    piece = piece + before[i][away, where, :]
                halves[i][away, where, :] = piece
            at = stop


def cost(us):
    return pl.CostEstimate(flops=0, bytes_accessed=int(us * 3.0e6), transcendentals=0)


VMEM = pl.BlockSpec(memory_space=pltpu.VMEM)
HBM = pl.BlockSpec(memory_space=pltpu.HBM)
SMEM = pl.BlockSpec(memory_space=pltpu.SMEM)
ANY = pl.BlockSpec(memory_space=pl.ANY)


class Chain:
    token = None

    def call(self, body, out_shape, scratch, us, *operands, in_specs=None, out_specs=None, alias=None, vmem=VMEM_LIMIT):
        def chained(*refs):
            after = refs[held + count]
            after[...] = refs[0][...] if held else jnp.zeros_like(after)
            body(*refs[held : held + count], *refs[held + count + 1 :])

        count, held = len(operands), int(self.token is not None)
        self.token, *outs = pl.pallas_call(
            chained,
            out_shape=(jax.ShapeDtypeStruct((8, LANES), F32), *out_shape),
            in_specs=[VMEM] * held + (in_specs or [VMEM] * count),
            out_specs=(VMEM, *(out_specs or [VMEM] * len(out_shape))),
            scratch_shapes=scratch,
            compiler_params=pltpu.CompilerParams(vmem_limit_bytes=vmem),
            cost_estimate=cost(us),
            input_output_aliases={i + held: o + 1 for i, o in (alias or {}).items()},
        )(*([self.token] * held), *operands)
        return outs


def add_kernel(up_offset, down_offset, first_terms, second_terms, first, second, first_out, second_out):
    first_out[...] = first_terms[up_offset] + first[...]
    second_out[...] = second_terms[down_offset] + second[...]


def final_kernel(first_terms, second_terms, first_up, first_down, second_down, second_up, out):
    out[:, :LANES] = first_terms[0] + first_up[...] + first_down[...]
    out[:, LANES:] = second_terms[0] + second_up[...] + second_down[...]


def shards(
    arriving_activations,
    fresh_images,
    saved_inputs,
    arriving_gradients,
    fresh_gradients,
    feed_order,
    forward_weight,
    forward_gain,
    forward_bias,
    backward_weight,
    backward_gain,
    backward_bias,
):
    ticks = saved_inputs.shape[0]
    d = Dims(*saved_inputs.shape[2:])
    sections = lax.axis_size("section")
    chips = sections // 2
    ring = [(i, (i + 1) % sections) for i in range(sections)]
    inside = [(i, i ^ 1) for i in range(sections)]

    act0 = interleaved(arriving_activations, d)
    grad0 = interleaved(arriving_gradients, d)
    fresh_act = interleaved(fresh_images, d)
    fresh_grad = interleaved(fresh_gradients, d)
    saved = interleaved(saved_inputs[:, 0], d)
    fgain, fbias, bgain, bbias = [
        v[0].reshape(d.cts, LANES) for v in (forward_gain, forward_bias, backward_gain, backward_bias)
    ]

    msg = jax.ShapeDtypeStruct((d.flat, LANES), F32)
    every = jax.ShapeDtypeStruct((ticks, d.flat, LANES), F32)
    rows = d.n * d.pix
    wide = jax.ShapeDtypeStruct((rows, d.c), F32)
    padded = pltpu.VMEM((d.padded, LANES), F32)
    cols = pltpu.VMEM((rows, 9 * d.c), BF16)
    flat = pltpu.VMEM((d.flat, LANES), F32)
    sem = pltpu.SemaphoreType.DMA

    whole = pltpu.VMEM((rows, d.c), F32)
    vector = pltpu.VMEM((d.cts, LANES), F32)
    narrow = jax.ShapeDtypeStruct((rows, d.c), BF16)
    raw = pltpu.VMEM((d.flat, LANES), BF16)

    last = ticks - 1

    def later(shape, dtype):
        return jax.ShapeDtypeStruct((last, *shape), dtype)

    chain = Chain()

    def first():
        return chain.call(
            functools.partial(first_kernel, d),
            (msg,),
            [raw, raw, vector, vector, pltpu.VMEM(backward_weight.shape[1:], BF16), whole, whole]
            + [pltpu.VMEM((rows, d.c), BF16), flat]
            + [padded] * 3
            + [cols, sem((5,))],
            2.5,
            saved,
            grad0,
            bgain,
            bbias,
            backward_weight[0],
            in_specs=[HBM] * 5,
            vmem=WHOLE_VMEM,
        )

    def prep():
        def all_ticks(shape, dtype, count=ticks):
            return jax.ShapeDtypeStruct((count, *shape), dtype)

        entering = all_ticks((d.flat, LANES), BF16, last)
        wide = all_ticks((rows, d.c), F32)
        return chain.call(
            functools.partial(prep_kernel, d),
            (wide, wide, all_ticks((8, LANES), F32), all_ticks((rows, d.c), BF16), entering, entering),
            [flat],
            2.0,
            feed_order,
            saved,
            bgain,
            bbias,
            fresh_act,
            fresh_grad,
            in_specs=[SMEM] + [VMEM] * 5,
        )

    def backward(slot, inner, outer):
        return chain.call(
            functools.partial(backward_kernel, d, slot),
            (msg, msg),
            [padded] * 3 + [cols],
            0.9,
            grad0,
            grads,
            inner,
            outer,
            slope,
            normed,
            rstd,
            backward_weight[0],
        )

    def forward(t, arrived, *collected):
        return chain.call(
            functools.partial(forward_kernel, d, t, chips, len(collected) - t if collected else 0),
            (msg, every, every) if collected else (msg,),
            [padded] * 3 + [cols, flat] + ([sem((2 * ticks,))] if collected else []),
            1.2,
            acts if t else act0,
            arrived,
            fgain,
            fbias,
            forward_weight[0],
            *collected,
            in_specs=[VMEM] * 5 + [ANY] * len(collected),
            out_specs=(VMEM, ANY, ANY) if collected else None,
        )

    n = lax.axis_size("dp")
    order = list(range(0, n, 2)) + list(range(n - 1 - n % 2, 0, -2))
    positions = [order.index(i) for i in range(n)]
    chunk = 9 * d.c // n
    half = jax.ShapeDtypeStruct((n, chunk, LANES), F32)

    def weight_terms(ticks, *operands):
        count = max(ticks, 1)
        return chain.call(
            functools.partial(weight_kernel, d, ticks, chips, n, positions, 1.0 / (n * d.n)),
            (half,) * 2,
            [flat] + [padded] * 3 + [pltpu.VMEM((count * rows, 9 * d.c), BF16)],
            0.6 * count,
            grad0,
            hidden,
            *operands,
            alias={} if ticks else {len(operands) + i: i for i in range(2)},
        )

    slots = ticks + chips - 1
    gradients, entered, inner, outer = first(), [None], [], []
    slope, normed, rstd, hidden, acts, grads = prep()
    arrived, outputs = jnp.zeros((8, LANES), F32), []

    def arrivals(slot):
        return inner[slot - 1], outer[max(slot - 2, 0)]

    for slot in range(slots - 1):
        if slot > 0:
            out, e = backward(slot, *arrivals(slot))
            gradients.append(out)
            entered.append(e)
        inner.append(lax.ppermute(gradients[slot], "section", inside))
        if slot < slots - 2:
            outer.append(lax.ppermute(gradients[slot], "section", ring))
        if slot == slots - 3:
            outputs += forward(0, arrived)
            arrived = lax.ppermute(outputs[0], "section", ring)
    before = weight_terms(last, *entered[1 : last + chips - 1])
    terms = weight_terms(0, grads, *arrivals(slots - 1), *entered[last : last + chips - 1], *before)

    onward = [(order[i], order[(i + 1) % n]) for i in range(n)]
    back = [(b, a) for a, b in onward]
    piece = jax.ShapeDtypeStruct((chunk, LANES), F32)
    hops = n // 2

    def swapped(first, second, ways):
        return [lax.ppermute(v, "dp", way) for v, way in zip((first, second), ways)]

    def long_hop(pair):
        return swapped(*pair, (onward, back))

    def short_hop(pair):
        return swapped(*pair, (back, onward))

    def added(pair, up, down):
        return chain.call(
            functools.partial(add_kernel, up % n, down % n), (piece,) * 2, [], 0.2, *terms, *pair
        )

    def forward_step(t, arrived):
        outputs.extend(forward(t, arrived))
        return lax.ppermute(outputs[t], "section", ring)

    long = long_hop([terms[0][hops], terms[1][n - hops]])
    short = short_hop([terms[0][n - hops + 1], terms[1][hops - 1]])
    arrived = forward_step(1, arrived)
    for hop in range(1, hops):
        long = long_hop(added(long, hops - hop, hop - hops))
        if hop < hops - 1:
            short = short_hop(added(short, hop + 1 - hops, hops - 1 - hop))
        if hop == 1:
            out, _ = backward(slots - 1, *arrivals(slots - 1))
            gradients.append(out)
        if 1 < hop < last:
            arrived = forward_step(hop, arrived)
    _, emitted, returned = forward(last, arrived, *outputs, *gradients)
    (shard_sum,) = chain.call(
        final_kernel, (jax.ShapeDtypeStruct((chunk, d.c), F32),), [], 0.4, *terms, *long[:1], *short[:1], *long[1:], *short[1:]
    )
    return standard(emitted, d)[:, None], standard(returned, d)[:, None], shard_sum[None]


def solution(mesh):
    placed = (
        P("section", "dp", None, None, None),
        P(None, "dp", None, None, None),
        P(None, "section", "dp", None, None, None),
        P("section", "dp", None, None, None),
        P(None, "dp", None, None, None),
        P(),
        P("section", None, None),
        P("section", None),
        P("section", None),
        P("section", None, None),
        P("section", None),
        P("section", None),
    )
    return jax.shard_map(
        shards,
        mesh=mesh,
        in_specs=placed,
        out_specs=(
            P(None, "section", "dp", None, None, None),
            P(None, "section", "dp", None, None, None),
            P("section", "dp", None),
        ),
        check_vma=False,
    )
```

```python
import functools
import math

import jax
import jax.numpy as jnp
from jax import lax
from jax.experimental import pallas as pl
from jax.experimental.pallas import tpu as pltpu
from jax.sharding import PartitionSpec as P

GROUPS = 32
F32 = jnp.float32
BF16 = jnp.bfloat16
LANES = 128
VMEM_LIMIT = 24 * 1024 * 1024
WHOLE_VMEM = 60 * 1024 * 1024


class Dims:
    def __init__(self, images, rows, cols, channels):
        self.n, self.h, self.w, self.c = images, rows, cols, channels
        self.cts = channels // LANES
        self.unit = self.cts * images
        self.pix = rows * cols
        self.flat = self.pix * self.unit
        per = 8 // math.gcd(8, self.unit)
        self.pad = -(-(cols + 1) // per) * per
        self.padded = (self.pix + 2 * self.pad) * self.unit
        self.count = self.pix * (channels // GROUPS)


def interleaved(x, d):
    lead = x.shape[:-4]
    k = len(lead)
    x = x.reshape(*lead, d.n, d.pix, d.cts, LANES)
    x = x.transpose(*range(k), k + 1, k + 2, k, k + 3)
    return x.reshape(*lead, d.flat, LANES)


def standard(x, d):
    lead = x.shape[:-2]
    k = len(lead)
    x = x.reshape(*lead, d.pix, d.cts, d.n, LANES)
    x = x.transpose(*range(k), k + 2, k, k + 1, k + 3)
    return x.reshape(*lead, d.n, d.h, d.w, d.c)


def group_sum(v, width):
    lane = lax.broadcasted_iota(jnp.int32, v.shape, 1)
    k = 1
    while k < width:
        v = v + jnp.where((lane & k) == 0, pltpu.roll(v, LANES - k, 1), pltpu.roll(v, k, 1))
        k *= 2
    return v


def pattern(ref, d):
    row = lax.broadcasted_iota(jnp.int32, (8, LANES), 0)
    ct = (row // d.n) % d.cts
    out = jnp.broadcast_to(ref[0:1, :], (8, LANES))
    for i in range(1, d.cts):
        out = jnp.where(ct == i, jnp.broadcast_to(ref[i : i + 1, :], (8, LANES)), out)
    return out


def unit_sum(v, d):
    s = jnp.sum(v, axis=0)
    k = d.unit
    while k < 8:
        s = s + pltpu.roll(s, k, 0)
        k *= 2
    return group_sum(s, d.c // GROUPS)


def normalized(x, d):
    tiles = x.reshape(-1, 8, LANES)
    scale = 1.0 / d.count
    mean = unit_sum(tiles, d) * scale
    centred = tiles - mean
    var = unit_sum(centred * centred, d) * scale
    rstd = lax.rsqrt(var + 1e-05)
    return centred * rstd, rstd


def sigmoid(a):
    return 0.5 * jnp.tanh(0.5 * a) + 0.5


def spread(value, refs, d):
    zeros = jnp.zeros((d.pad * d.unit, LANES), F32)
    for ref in refs:
        ref[0 : d.pad * d.unit, :] = zeros
        ref[d.padded - d.pad * d.unit : d.padded, :] = zeros
        ref[d.pad * d.unit : d.pad * d.unit + d.flat, :] = value
    edge = jnp.zeros((d.unit, LANES), F32)
    for i in range(d.h):
        last = (d.pad + i * d.w + d.w - 1) * d.unit
        first = (d.pad + i * d.w) * d.unit
        refs[0][last : last + d.unit, :] = edge
        refs[2][first : first + d.unit, :] = edge


def plane(ref, d, shift, n):
    parts = [
        ref[pl.ds((d.pad + shift) * d.unit + ct * d.n + n, d.pix, stride=d.unit), :] for ct in range(d.cts)
    ]
    return jnp.concatenate(parts, axis=1)


def gather_patches(refs, out_ref, d):
    for kr in range(3):
        for kc in range(3):
            tap = kr * 3 + kc
            for n in range(d.n):
                block = plane(refs[kc], d, (kr - 1) * d.w + kc - 1, n)
                out_ref[n * d.pix : (n + 1) * d.pix, tap * d.c : (tap + 1) * d.c] = block.astype(BF16)


def from_interleaved(ref, d, base=0):
    rows = [
        jnp.concatenate(
            [ref[pl.ds(base + ct * d.n + n, d.pix, stride=d.unit), :] for ct in range(d.cts)], axis=1
        )
        for n in range(d.n)
    ]
    return jnp.concatenate(rows, axis=0)


def to_interleaved(ref, n, value, d):
    for ct in range(d.cts):
        ref[pl.ds(ct * d.n + n, d.pix, stride=d.unit), :] = value[:, ct * LANES : (ct + 1) * LANES]


def prepare(d, x, gain_ref, bias_ref, slope_ref, normed_ref, hidden_ref, tmp):
    normed, rstd = normalized(x, d)
    gain = pattern(gain_ref, d)
    a = normed * gain + pattern(bias_ref, d)
    s = sigmoid(a)
    for ref, value in (
        (normed_ref, normed),
        (slope_ref, s * (1.0 + a * (1.0 - s)) * gain),
        (hidden_ref, a * s),
    ):
        tmp[...] = value.reshape(d.flat, LANES)
        ref[...] = from_interleaved(tmp, d).astype(ref.dtype)
    return rstd


def prep_kernel(d, slot, saved_ref, gain_ref, bias_ref, slope_ref, normed_ref, rstd_ref, hidden_ref, tmp):
    t = jnp.minimum(jnp.maximum(slot - chip(), 0), saved_ref.shape[0] - 1)
    rstd_ref[...] = prepare(d, saved_ref[t].astype(F32), gain_ref, bias_ref, slope_ref, normed_ref, hidden_ref, tmp)


def picked(feed_ref, tick, fresh_ref):
    index = feed_ref[:, tick - 1 : tick]
    out = fresh_ref[0].astype(F32)
    for k in range(1, fresh_ref.shape[0]):
        out = jnp.where(index == k, fresh_ref[k].astype(F32), out)
    return out


def through_layer(d, cols, weight_ref, slope_ref, normed_ref, rstd, mid, out_ref):
    grad = None
    for tap in range(9):
        part = lax.dot_general(
            cols[:, tap * d.c : (tap + 1) * d.c],
            weight_ref[(8 - tap) * d.c : (9 - tap) * d.c, :],
            (((1,), (1,)), ((), ())),
            preferred_element_type=F32,
        )
        grad = part if grad is None else grad + part
    through = grad * slope_ref[...]
    weighted = through * normed_ref[...]
    rows = []
    for ct in range(d.cts):
        for n in range(d.n):
            for v in (through, weighted):
                rows.append(
                    jnp.sum(v[n * d.pix : (n + 1) * d.pix, ct * LANES : (ct + 1) * LANES], axis=0, keepdims=True)
                )
    sums = group_sum(jnp.concatenate(rows, axis=0), d.c // GROUPS) * (1.0 / d.count)
    for n in range(d.n):
        for ct in range(d.cts):
            where = ct * d.n + n
            k = where * 2
            here = (slice(n * d.pix, (n + 1) * d.pix), slice(ct * LANES, (ct + 1) * LANES))
            value = (through[here] - sums[k : k + 1] - normed_ref[here] * sums[k + 1 : k + 2]) * rstd[where : where + 1, :]
            e_here = mid[pl.ds(d.pad * d.unit + where, d.pix, stride=d.unit), :]
            out_ref[pl.ds(where, d.pix, stride=d.unit), :] = value + e_here


def first_kernel(d, saved_hbm, grad_hbm, gain_hbm, bias_hbm, weight_hbm, *refs):
    out_ref, hidden, saved, grad, gain, bias, weight, slope, normed, tmp, left, mid, right, cols, sems = refs

    @pl.when(chip() == 0)
    def _():
        pairs = [(grad_hbm.at[0], grad), (saved_hbm.at[0], saved), (gain_hbm, gain), (bias_hbm, bias), (weight_hbm, weight)]
        copies = [pltpu.make_async_copy(src, dst, sems.at[i]) for i, (src, dst) in enumerate(pairs)]
        for copy in copies:
            copy.start()
        copies[0].wait()
        spread(grad[...].astype(F32), (left, mid, right), d)
        gather_patches((left, mid, right), cols, d)
        for copy in copies[1:4]:
            copy.wait()
        rstd = prepare(d, saved[...].astype(F32), gain, bias, slope, normed, hidden, tmp)
        copies[4].wait()
        through_layer(d, cols, weight, slope, normed, rstd, mid, out_ref)

    @pl.when(chip() != 0)
    def _():
        out_ref[...] = jnp.zeros_like(out_ref)
        hidden[...] = jnp.zeros_like(hidden)


def chip():
    return lax.axis_index("section") // 2


def enter(slot, grad0_ref, feed_ref, fresh_ref, inner_ref, outer_ref, e_ref):
    tick = slot - chip()
    second = lax.axis_index("section") % 2 == 1

    @pl.when(tick == 0)
    def _():
        e_ref[...] = grad0_ref[0].astype(F32)

    @pl.when(jnp.logical_and(tick > 0, second))
    def _():
        e_ref[...] = inner_ref[...]

    @pl.when(jnp.logical_and(tick > 0, jnp.logical_and(jnp.logical_not(second), chip() > 0)))
    def _():
        e_ref[...] = outer_ref[...]

    if 0 < slot <= feed_ref.shape[1]:

        @pl.when(lax.axis_index("section") == 0)
        def _():
            e_ref[...] = picked(feed_ref, slot, fresh_ref)


def backward_kernel(
    d, slot, grad0_ref, feed_ref, fresh_ref, inner_ref, outer_ref, slope_ref, normed_ref, rstd_ref, weight_ref, *refs
):
    out_ref, e_ref, left, mid, right, cols = refs
    tick = slot - chip()
    runs = jnp.logical_and(tick >= 0, tick <= feed_ref.shape[1])

    @pl.when(runs)
    def _():
        enter(slot, grad0_ref, feed_ref, fresh_ref, inner_ref, outer_ref, e_ref)
        spread(e_ref[...], (left, mid, right), d)
        gather_patches((left, mid, right), cols, d)
        through_layer(d, cols, weight_ref, slope_ref, normed_ref, rstd_ref[...], mid, out_ref)

    @pl.when(jnp.logical_not(runs))
    def _():
        out_ref[...] = jnp.zeros_like(out_ref)
        e_ref[...] = jnp.zeros_like(e_ref)


def forward_kernel(d, tick, feed_ref, fresh_ref, arrived_ref, gain_ref, bias_ref, weight_ref, *refs):
    out_ref, left, mid, right, cols, kept = refs
    if tick == 0:
        x = fresh_ref[0].astype(F32)
        kept[...] = x
    else:
        section = lax.axis_index("section")

        @pl.when(section == 0)
        def _():
            kept[...] = picked(feed_ref, tick, fresh_ref)

        @pl.when(section != 0)
        def _():
            kept[...] = arrived_ref[...]

        x = kept[...]
    normed, _ = normalized(x, d)
    a = normed * pattern(gain_ref, d) + pattern(bias_ref, d)
    hidden = (a * sigmoid(a)).reshape(d.flat, LANES)
    spread(hidden, (left, mid, right), d)
    gather_patches((left, mid, right), cols, d)
    conv = jnp.dot(cols[...], weight_ref[...], preferred_element_type=F32)
    for n in range(d.n):
        for ct in range(d.cts):
            where = pl.ds(ct * d.n + n, d.pix, stride=d.unit)
            out_ref[where, :] = (
                kept[where, :] + conv[n * d.pix : (n + 1) * d.pix, ct * LANES : (ct + 1) * LANES]
            )


def weight_kernel(d, ticks, first, chips, n, positions, factor, grad0_ref, feed_ref, fresh_ref, inner_ref, outer_ref, *refs):
    me = lax.axis_index("dp")
    here = jnp.where(me % 2 == 0, me // 2, n - 1 - me // 2)
    rows = d.n * d.pix
    chunk = 9 * d.c // n
    last = feed_ref.shape[1]
    slots = last + chips
    span = len(ticks) + chips - 1
    hidden_refs, refs = refs[:span], refs[span:]
    e_refs, refs = refs[:span], refs[span:]
    before, refs = (None, refs) if first else (refs[:2], refs[2:])
    halves, (kept, left, mid, right, cols, hid) = refs[:2], refs[2:]
    for i, t in enumerate(ticks):
        if t == 0:
            kept[...] = grad0_ref[0].astype(F32)
        for c in range(chips):

            @pl.when(chip() == c)
            def _():
                hid[i * rows : (i + 1) * rows, :] = hidden_refs[i + c][...]
                if t + c == slots - 1:
                    enter(slots - 1, grad0_ref, feed_ref, fresh_ref, inner_ref, outer_ref, kept)
                elif t > 0:
                    kept[...] = e_refs[i + c][...]

        spread(kept[...], (left, mid, right), d)
        gather_patches((left, mid, right), cols.at[i * rows : (i + 1) * rows], d)
    h = hid[...]
    for tap in range(9):
        block = lax.dot_general(
            h, cols[:, (8 - tap) * d.c : (9 - tap) * d.c], (((0,), (0,)), ((), ())), preferred_element_type=F32
        ) * factor
        at = tap * d.c
        while at < (tap + 1) * d.c:
            owner = at // chunk
            stop = min((owner + 1) * chunk, (tap + 1) * d.c)
            where = pl.ds(at - owner * chunk, stop - at)
            away = (positions[owner] - here + n) % n
            for i in range(2):
                piece = block[at - tap * d.c : stop - tap * d.c, i * LANES : (i + 1) * LANES]
                if not first:
                    piece = piece + before[i][away, where, :]
                halves[i][away, where, :] = piece
            at = stop


def cost(weight):
    return pl.CostEstimate(flops=weight * 10**9, bytes_accessed=0, transcendentals=0)


VMEM = pl.BlockSpec(memory_space=pltpu.VMEM)
HBM = pl.BlockSpec(memory_space=pltpu.HBM)
SMEM = pl.BlockSpec(memory_space=pltpu.SMEM)
ANY = pl.BlockSpec(memory_space=pl.ANY)


class Chain:
    def __init__(self, chips, every):
        self.chips, self.every = chips, every
        self.tokens = []
        self.kept = {}

    def call(
        self,
        body,
        out_shape,
        scratch,
        weight,
        *operands,
        in_specs=None,
        alias=None,
        vmem=VMEM_LIMIT,
        follows=True,
        passed=(),
        stores=(),
        own=None,
    ):
        tokens = self.tokens if follows else []
        names = sorted({s[0] for s in stores} | ({own[0]} if own else set()))
        sources = [v for s in stores for v in s[2]]
        old = [self.kept[k] for k in names if k in self.kept]
        counts = [len(tokens), len(operands), len(passed), len(sources), len(old), 1, len(out_shape), len(passed), len(names)]
        starts = [sum(counts[:i]) for i in range(len(counts) + 1)]

        def chained(*refs):
            groups = [refs[starts[i] : starts[i + 1]] for i in range(len(counts))]
            rest = refs[starts[-1] :]
            outs, kept = groups[6], dict(zip(names, groups[8]))
            waits = []

            def send(source, name, tick, sem):
                copy = pltpu.make_async_copy(source, kept[name].at[tick], sem)
                copy.start()
                return copy

            if names:
                *rest, sems = rest
                from_refs = list(groups[3])
                for i, (name, tick, per_chip) in enumerate(stores):
                    mine, from_refs = from_refs[: len(per_chip)], from_refs[len(per_chip) :]
                    if len(mine) == 1:
                        waits.append(send(mine[0], name, tick, sems.at[i]))
                        continue
                    for c in range(len(mine)):

                        @pl.when(chip() == c)
                        def _():
                            send(mine[c], name, tick, sems.at[i])

                    waits.append(pltpu.make_async_copy(mine[0], kept[name].at[tick], sems.at[i]))
            total = jnp.zeros((8, LANES), F32)
            for ref in groups[0]:
                total = total + ref[...]
            groups[5][0][...] = total
            body(*groups[1], *outs, *rest)
            if own:
                name, tick, where = own
                if where is None:
                    waits.append(send(outs[0], name, tick, sems.at[len(stores)]))
                else:

                    @pl.when(chip() == where)
                    def _():
                        send(outs[0], name, tick, sems.at[len(stores)]).wait()

            for copy in waits:
                copy.wait()

        aliases = {starts[1] + i: starts[6] - starts[5] + o for i, o in (alias or {}).items()}
        aliases |= {starts[2] + i: 1 + len(out_shape) + i for i in range(len(passed))}
        aliases |= {
            starts[4] + i: 1 + len(out_shape) + len(passed) + names.index(k)
            for i, k in enumerate([k for k in names if k in self.kept])
        }
        token, *outs = pl.pallas_call(
            chained,
            out_shape=(
                jax.ShapeDtypeStruct((8, LANES), F32),
                *out_shape,
                *[jax.ShapeDtypeStruct(v.shape, v.dtype) for v in passed],
                *[self.every] * len(names),
            ),
            in_specs=[VMEM] * len(tokens)
            + (in_specs or [VMEM] * len(operands))
            + [VMEM] * len(passed)
            + [ANY] * (len(sources) + len(old)),
            out_specs=[VMEM] * (1 + len(out_shape) + len(passed)) + [ANY] * len(names),
            scratch_shapes=[*scratch] + ([pltpu.SemaphoreType.DMA((len(stores) + 1,))] if names else []),
            compiler_params=pltpu.CompilerParams(vmem_limit_bytes=vmem),
            cost_estimate=cost(weight),
            input_output_aliases=aliases,
        )(*tokens, *operands, *passed, *sources, *old)
        self.tokens = [token] if follows else self.tokens + [token]
        for k, v in zip(names, outs[len(out_shape) + len(passed) :]):
            self.kept[k] = v
        return outs[: len(out_shape) + len(passed)]


def add_kernel(up_offset, down_offset, first_terms, second_terms, first, second, first_out, second_out):
    first_out[...] = first_terms[up_offset] + first[...]
    second_out[...] = second_terms[down_offset] + second[...]


def final_kernel(first_terms, second_terms, first_up, first_down, second_down, second_up, out):
    out[:, :LANES] = first_terms[0] + first_up[...] + first_down[...]
    out[:, LANES:] = second_terms[0] + second_up[...] + second_down[...]


def shards(
    arriving_activations,
    fresh_images,
    saved_inputs,
    arriving_gradients,
    fresh_gradients,
    feed_order,
    forward_weight,
    forward_gain,
    forward_bias,
    backward_weight,
    backward_gain,
    backward_bias,
):
    ticks = saved_inputs.shape[0]
    d = Dims(*saved_inputs.shape[2:])
    sections = lax.axis_size("section")
    chips = sections // 2
    ring = [(i, (i + 1) % sections) for i in range(sections)]
    inside = [(i, i ^ 1) for i in range(sections)]

    act0 = interleaved(arriving_activations, d)
    grad0 = interleaved(arriving_gradients, d)
    fresh_act = interleaved(fresh_images, d)
    fresh_grad = interleaved(fresh_gradients, d)
    saved = interleaved(saved_inputs[:, 0], d)
    feed = feed_order.reshape(1, -1)
    fgain, fbias, bgain, bbias = [
        v[0].reshape(d.cts, LANES) for v in (forward_gain, forward_bias, backward_gain, backward_bias)
    ]

    msg = jax.ShapeDtypeStruct((d.flat, LANES), F32)
    every = jax.ShapeDtypeStruct((ticks, d.flat, LANES), F32)
    rows = d.n * d.pix
    wide = jax.ShapeDtypeStruct((rows, d.c), F32)
    padded = pltpu.VMEM((d.padded, LANES), F32)
    cols = pltpu.VMEM((rows, 9 * d.c), BF16)
    flat = pltpu.VMEM((d.flat, LANES), F32)
    sem = pltpu.SemaphoreType.DMA

    whole = pltpu.VMEM((rows, d.c), F32)
    vector = pltpu.VMEM((d.cts, LANES), F32)
    narrow = jax.ShapeDtypeStruct((rows, d.c), BF16)
    raw = pltpu.VMEM((d.flat, LANES), BF16)

    last = ticks - 1

    def later(shape, dtype):
        return jax.ShapeDtypeStruct((last, *shape), dtype)

    chain = Chain(chips, every)

    def first():
        return chain.call(
            functools.partial(first_kernel, d),
            (msg, narrow),
            [raw, raw, vector, vector, pltpu.VMEM(backward_weight.shape[1:], BF16), whole, whole, flat]
            + [padded] * 3
            + [cols, sem((5,))],
            0,
            saved,
            grad0,
            bgain,
            bbias,
            backward_weight[0],
            in_specs=[HBM] * 5,
            vmem=WHOLE_VMEM,
        )

    def prep(slot):
        return chain.call(
            functools.partial(prep_kernel, d, slot),
            (wide, wide, jax.ShapeDtypeStruct((8, LANES), F32), narrow),
            [flat],
            0,
            saved,
            bgain,
            bbias,
        )

    def backward(slot, inner, outer, slope, normed, rstd, **more):
        return chain.call(
            functools.partial(backward_kernel, d, slot),
            (msg, msg),
            [padded] * 3 + [cols],
            0,
            grad0,
            feed,
            fresh_grad,
            inner,
            outer,
            slope,
            normed,
            rstd,
            backward_weight[0],
            **more,
        )

    def forward(t, arrived, **more):
        return chain.call(
            functools.partial(forward_kernel, d, t),
            (msg,),
            [padded] * 3 + [cols, flat],
            0,
            feed,
            fresh_act if t else act0,
            arrived,
            fgain,
            fbias,
            forward_weight[0],
            **more,
        )

    n = lax.axis_size("dp")
    order = list(range(0, n, 2)) + list(range(n - 1 - n % 2, 0, -2))
    positions = [order.index(i) for i in range(n)]
    chunk = 9 * d.c // n
    half = jax.ShapeDtypeStruct((n, chunk, LANES), F32)

    def weight_terms(ticks, inner, outer, *before, passed=()):
        span = slice(ticks[0], ticks[-1] + chips)
        operands = hidden[span] + [e if e is not None else grad0 for e in (entered + [None])[span]]
        return chain.call(
            functools.partial(weight_kernel, d, ticks, not before, chips, n, positions, 1.0 / (n * d.n)),
            (half,) * 2,
            [flat]
            + [padded] * 3
            + [pltpu.VMEM((len(ticks) * rows, 9 * d.c), BF16), pltpu.VMEM((len(ticks) * rows, d.c), BF16)],
            0,
            grad0,
            feed,
            fresh_grad,
            inner,
            outer,
            *operands,
            *before,
            alias={5 + len(operands) + i: i for i in range(len(before))},
            passed=passed,
        )

    slots = ticks + chips - 1
    out, h = first()
    gradients, hidden, entered, inner, outer = [out], [h], [None], [], []
    outputs = []

    def arrivals(slot):
        return inner[slot - 1], outer[slot - 2] if slot > 1 else inner[0]

    prepared = [None]
    for slot in range(slots - 1):
        if slot > 0:
            out, e = backward(slot, *arrivals(slot), *prepared[slot])
            gradients.append(out)
            entered.append(e)
        inner.append(lax.ppermute(gradients[slot], "section", inside))
        if slot < slots - 2:
            outer.append(lax.ppermute(gradients[slot], "section", ring))
            *ready, h = prep(slot + 1)
            prepared.append(ready)
            hidden.append(h)
        if slot == slots - 3:
            outputs += forward(0, inner[0])
            arrived = lax.ppermute(outputs[0], "section", ring)
            *ready, h = prep(slot + 2)
            prepared.append(ready)
            hidden.append(h)
    terms = weight_terms(range(last), inner[0], inner[0])
    terms = weight_terms([last], *arrivals(slots - 1), *terms)

    onward = [(order[i], order[(i + 1) % n]) for i in range(n)]
    back = [(b, a) for a, b in onward]
    piece = jax.ShapeDtypeStruct((chunk, LANES), F32)
    hops = n // 2

    def swapped(first, second, ways):
        return [lax.ppermute(v, "dp", way) for v, way in zip((first, second), ways)]

    def long_hop(pair):
        return swapped(*pair, (onward, back))

    def short_hop(pair):
        return swapped(*pair, (back, onward))

    def added(pair, up, down):
        return chain.call(
            functools.partial(add_kernel, up % n, down % n), (piece,) * 2, [], 3, *terms, *pair
        )

    def returned(t):
        return ("returned", t, gradients[t : t + chips])

    def emitted(t):
        return ("emitted", t, outputs[t : t + 1])

    def forward_step(t, arrived, **more):
        outputs.extend(forward(t, arrived, **more))
        return lax.ppermute(outputs[t], "section", ring)

    long = long_hop([terms[0][hops], terms[1][n - hops]])
    short = short_hop([terms[0][n - hops + 1], terms[1][hops - 1]])
    arrived = forward_step(1, arrived, stores=[emitted(0)] + [returned(t) for t in range(last - 1)])
    for hop in range(1, hops):
        long = long_hop(added(long, hops - hop, hop - hops))
        if hop < hops - 1:
            short = short_hop(added(short, hop + 1 - hops, hops - 1 - hop))
        if hop < last - 1:
            arrived = forward_step(hop + 1, arrived, stores=[emitted(hop), returned(last - 1)] if hop == 1 else [emitted(hop)])
        if hop == last - 1:
            out, _ = backward(slots - 1, *arrivals(slots - 1), *prepared[slots - 1], stores=[emitted(last - 1)])
            gradients.append(out)
    forward(last, arrived, stores=[returned(last)], own=("emitted", last, None))
    (shard_sum,) = chain.call(
        final_kernel, (jax.ShapeDtypeStruct((chunk, d.c), F32),), [], 0, *terms, *long[:1], *short[:1], *long[1:], *short[1:]
    )
    return (
        standard(chain.kept["emitted"], d)[:, None],
        standard(chain.kept["returned"], d)[:, None],
        shard_sum[None],
    )


def solution(mesh):
    placed = (
        P("section", "dp", None, None, None),
        P(None, "dp", None, None, None),
        P(None, "section", "dp", None, None, None),
        P("section", "dp", None, None, None),
        P(None, "dp", None, None, None),
        P(),
        P("section", None, None),
        P("section", None),
        P("section", None),
        P("section", None, None),
        P("section", None),
        P("section", None),
    )
    return jax.shard_map(
        shards,
        mesh=mesh,
        in_specs=placed,
        out_specs=(
            P(None, "section", "dp", None, None, None),
            P(None, "section", "dp", None, None, None),
            P("section", "dp", None),
        ),
        check_vma=False,
    )
```

```python
import functools
import math

import jax
import jax.numpy as jnp
from jax import lax
from jax.experimental import pallas as pl
from jax.experimental.pallas import tpu as pltpu
from jax.sharding import PartitionSpec as P

GROUPS = 32
F32 = jnp.float32
BF16 = jnp.bfloat16
LANES = 128
VMEM_LIMIT = 24 * 1024 * 1024
WHOLE_VMEM = 60 * 1024 * 1024


class Dims:
    def __init__(self, images, rows, cols, channels):
        self.n, self.h, self.w, self.c = images, rows, cols, channels
        self.cts = channels // LANES
        self.unit = self.cts * images
        self.pix = rows * cols
        self.flat = self.pix * self.unit
        per = 8 // math.gcd(8, self.unit)
        self.pad = -(-(cols + 1) // per) * per
        self.padded = (self.pix + 2 * self.pad) * self.unit
        self.count = self.pix * (channels // GROUPS)


def interleaved(x, d):
    lead = x.shape[:-4]
    k = len(lead)
    x = x.reshape(*lead, d.n, d.pix, d.cts, LANES)
    x = x.transpose(*range(k), k + 1, k + 2, k, k + 3)
    return x.reshape(*lead, d.flat, LANES)


def standard(x, d):
    lead = x.shape[:-2]
    k = len(lead)
    x = x.reshape(*lead, d.pix, d.cts, d.n, LANES)
    x = x.transpose(*range(k), k + 2, k, k + 1, k + 3)
    return x.reshape(*lead, d.n, d.h, d.w, d.c)


def group_sum(v, width):
    lane = lax.broadcasted_iota(jnp.int32, v.shape, 1)
    k = 1
    while k < width:
        v = v + jnp.where((lane & k) == 0, pltpu.roll(v, LANES - k, 1), pltpu.roll(v, k, 1))
        k *= 2
    return v


def pattern(ref, d):
    row = lax.broadcasted_iota(jnp.int32, (8, LANES), 0)
    ct = (row // d.n) % d.cts
    out = jnp.broadcast_to(ref[0:1, :], (8, LANES))
    for i in range(1, d.cts):
        out = jnp.where(ct == i, jnp.broadcast_to(ref[i : i + 1, :], (8, LANES)), out)
    return out


def unit_sum(v, d):
    s = jnp.sum(v, axis=0)
    k = d.unit
    while k < 8:
        s = s + pltpu.roll(s, k, 0)
        k *= 2
    return group_sum(s, d.c // GROUPS)


def normalized(x, d):
    tiles = x.reshape(-1, 8, LANES)
    scale = 1.0 / d.count
    mean = unit_sum(tiles, d) * scale
    centred = tiles - mean
    var = unit_sum(centred * centred, d) * scale
    rstd = lax.rsqrt(var + 1e-05)
    return centred * rstd, rstd


def sigmoid(a):
    return 0.5 * jnp.tanh(0.5 * a) + 0.5


def spread(value, refs, d):
    zeros = jnp.zeros((d.pad * d.unit, LANES), F32)
    for ref in refs:
        ref[0 : d.pad * d.unit, :] = zeros
        ref[d.padded - d.pad * d.unit : d.padded, :] = zeros
        ref[d.pad * d.unit : d.pad * d.unit + d.flat, :] = value
    edge = jnp.zeros((d.unit, LANES), F32)
    for i in range(d.h):
        last = (d.pad + i * d.w + d.w - 1) * d.unit
        first = (d.pad + i * d.w) * d.unit
        refs[0][last : last + d.unit, :] = edge
        refs[2][first : first + d.unit, :] = edge


def plane(ref, d, shift, n):
    parts = [
        ref[pl.ds((d.pad + shift) * d.unit + ct * d.n + n, d.pix, stride=d.unit), :] for ct in range(d.cts)
    ]
    return jnp.concatenate(parts, axis=1)


def gather_patches(refs, out_ref, d):
    for kr in range(3):
        for kc in range(3):
            tap = kr * 3 + kc
            for n in range(d.n):
                block = plane(refs[kc], d, (kr - 1) * d.w + kc - 1, n)
                out_ref[n * d.pix : (n + 1) * d.pix, tap * d.c : (tap + 1) * d.c] = block.astype(BF16)


def from_interleaved(ref, d, base=0):
    rows = [
        jnp.concatenate(
            [ref[pl.ds(base + ct * d.n + n, d.pix, stride=d.unit), :] for ct in range(d.cts)], axis=1
        )
        for n in range(d.n)
    ]
    return jnp.concatenate(rows, axis=0)


def to_interleaved(ref, n, value, d):
    for ct in range(d.cts):
        ref[pl.ds(ct * d.n + n, d.pix, stride=d.unit), :] = value[:, ct * LANES : (ct + 1) * LANES]


def prepare(d, x, gain_ref, bias_ref, slope_ref, normed_ref, hidden_ref, tmp):
    normed, rstd = normalized(x, d)
    gain = pattern(gain_ref, d)
    a = normed * gain + pattern(bias_ref, d)
    s = sigmoid(a)
    for ref, value in (
        (normed_ref, normed),
        (slope_ref, s * (1.0 + a * (1.0 - s)) * gain),
        (hidden_ref, a * s),
    ):
        tmp[...] = value.reshape(d.flat, LANES)
        ref[...] = from_interleaved(tmp, d).astype(ref.dtype)
    return rstd


def prep_kernel(d, slot, saved_ref, gain_ref, bias_ref, slope_ref, normed_ref, rstd_ref, hidden_ref, tmp):
    tick = slot - chip()
    last = saved_ref.shape[0] - 1

    @pl.when(jnp.logical_and(tick >= 1, tick <= last))
    def _():
        x = saved_ref[jnp.minimum(jnp.maximum(tick, 1), last)].astype(F32)
        rstd_ref[...] = prepare(d, x, gain_ref, bias_ref, slope_ref, normed_ref, hidden_ref, tmp)


def picked(feed_ref, tick, fresh_ref):
    index = feed_ref[:, tick - 1 : tick]
    out = fresh_ref[0].astype(F32)
    for k in range(1, fresh_ref.shape[0]):
        out = jnp.where(index == k, fresh_ref[k].astype(F32), out)
    return out


def through_layer(d, cols, weight_ref, slope_ref, normed_ref, rstd, mid, out_ref):
    grad = None
    for tap in range(9):
        part = lax.dot_general(
            cols[:, tap * d.c : (tap + 1) * d.c],
            weight_ref[(8 - tap) * d.c : (9 - tap) * d.c, :],
            (((1,), (1,)), ((), ())),
            preferred_element_type=F32,
        )
        grad = part if grad is None else grad + part
    through = grad * slope_ref[...]
    weighted = through * normed_ref[...]
    rows = []
    for ct in range(d.cts):
        for n in range(d.n):
            for v in (through, weighted):
                rows.append(
                    jnp.sum(v[n * d.pix : (n + 1) * d.pix, ct * LANES : (ct + 1) * LANES], axis=0, keepdims=True)
                )
    sums = group_sum(jnp.concatenate(rows, axis=0), d.c // GROUPS) * (1.0 / d.count)
    for n in range(d.n):
        for ct in range(d.cts):
            where = ct * d.n + n
            k = where * 2
            here = (slice(n * d.pix, (n + 1) * d.pix), slice(ct * LANES, (ct + 1) * LANES))
            value = (through[here] - sums[k : k + 1] - normed_ref[here] * sums[k + 1 : k + 2]) * rstd[where : where + 1, :]
            e_here = mid[pl.ds(d.pad * d.unit + where, d.pix, stride=d.unit), :]
            out_ref[pl.ds(where, d.pix, stride=d.unit), :] = value + e_here


def first_kernel(d, saved_hbm, grad_hbm, gain_hbm, bias_hbm, weight_hbm, *refs):
    out_ref, hidden, saved, grad, gain, bias, weight, slope, normed, tmp, left, mid, right, cols, sems = refs
    pairs = [(grad_hbm.at[0], grad), (saved_hbm.at[0], saved), (gain_hbm, gain), (bias_hbm, bias), (weight_hbm, weight)]
    copies = [pltpu.make_async_copy(src, dst, sems.at[i]) for i, (src, dst) in enumerate(pairs)]
    for copy in copies:
        copy.start()
    copies[0].wait()
    spread(grad[...].astype(F32), (left, mid, right), d)
    gather_patches((left, mid, right), cols, d)
    for copy in copies[1:4]:
        copy.wait()
    rstd = prepare(d, saved[...].astype(F32), gain, bias, slope, normed, hidden, tmp)
    copies[4].wait()
    through_layer(d, cols, weight, slope, normed, rstd, mid, out_ref)


def chip():
    return lax.axis_index("section") // 2


def enter(slot, feed_ref, fresh_ref, inner0_ref, inner_ref, outer0_ref, outer_ref, e_ref):
    tick = slot - chip()
    second = lax.axis_index("section") % 2 == 1
    beyond = jnp.logical_and(jnp.logical_not(second), chip() > 0)

    for condition, ref in (
        (jnp.logical_and(second, tick == 1), inner0_ref),
        (jnp.logical_and(second, tick > 1), inner_ref),
        (jnp.logical_and(beyond, tick == 1), outer0_ref),
        (jnp.logical_and(beyond, tick > 1), outer_ref),
    ):

        @pl.when(condition)
        def _():
            e_ref[...] = ref[...]

    if slot <= feed_ref.shape[1]:

        @pl.when(lax.axis_index("section") == 0)
        def _():
            e_ref[...] = picked(feed_ref, slot, fresh_ref)


def backward_kernel(d, slot, feed_ref, fresh_ref, *refs):
    arrived, (slope_ref, normed_ref, rstd_ref, weight_ref), refs = refs[:4], refs[4:8], refs[8:]
    out_ref, e_ref, left, mid, right, cols = refs
    tick = slot - chip()
    runs = jnp.logical_and(tick >= 1, tick <= feed_ref.shape[1])

    @pl.when(runs)
    def _():
        enter(slot, feed_ref, fresh_ref, *arrived, e_ref)
        spread(e_ref[...], (left, mid, right), d)
        gather_patches((left, mid, right), cols, d)
        through_layer(d, cols, weight_ref, slope_ref, normed_ref, rstd_ref[...], mid, out_ref)

    @pl.when(jnp.logical_not(runs))
    def _():
        out_ref[...] = jnp.zeros_like(out_ref)
        e_ref[...] = jnp.zeros_like(e_ref)


def forward_kernel(d, tick, feed_ref, fresh_ref, arrived_ref, gain_ref, bias_ref, weight_ref, *refs):
    out_ref, left, mid, right, cols, kept = refs
    if tick == 0:
        x = fresh_ref[0].astype(F32)
        kept[...] = x
    else:
        section = lax.axis_index("section")

        @pl.when(section == 0)
        def _():
            kept[...] = picked(feed_ref, tick, fresh_ref)

        @pl.when(section != 0)
        def _():
            kept[...] = arrived_ref[...]

        x = kept[...]
    normed, _ = normalized(x, d)
    a = normed * pattern(gain_ref, d) + pattern(bias_ref, d)
    hidden = (a * sigmoid(a)).reshape(d.flat, LANES)
    spread(hidden, (left, mid, right), d)
    gather_patches((left, mid, right), cols, d)
    conv = jnp.dot(cols[...], weight_ref[...], preferred_element_type=F32)
    for n in range(d.n):
        for ct in range(d.cts):
            where = pl.ds(ct * d.n + n, d.pix, stride=d.unit)
            out_ref[where, :] = (
                kept[where, :] + conv[n * d.pix : (n + 1) * d.pix, ct * LANES : (ct + 1) * LANES]
            )


def weight_kernel(d, ticks, first, chips, n, positions, factor, slots, grad0_ref, feed_ref, fresh_ref, *refs):
    me = lax.axis_index("dp")
    here = jnp.where(me % 2 == 0, me // 2, n - 1 - me // 2)
    rows = d.n * d.pix
    chunk = 9 * d.c // n
    last = feed_ref.shape[1]
    arrived, refs = refs[:4], refs[4:]
    hidden_refs, refs = dict(zip(slots, refs)), refs[len(slots) :]
    e_refs, refs = dict(zip(slots, refs)), refs[len(slots) :]
    before, refs = (None, refs) if first else (refs[:2], refs[2:])
    halves, first_short, (kept, left, mid, right, cols, hid) = refs[:2], refs[2:-6], refs[-6:]
    for i, t in enumerate(ticks):
        if t == 0:
            kept[...] = grad0_ref[0].astype(F32)
            hid[i * rows : (i + 1) * rows, :] = hidden_refs[0][...]
        for c in range(chips if t else 0):

            @pl.when(chip() == c)
            def _():
                hid[i * rows : (i + 1) * rows, :] = hidden_refs[t + c][...]
                if t + c == last + chips - 1:
                    enter(t + c, feed_ref, fresh_ref, *arrived, kept)
                else:
                    kept[...] = e_refs[t + c][...]

        spread(kept[...], (left, mid, right), d)
        gather_patches((left, mid, right), cols.at[i * rows : (i + 1) * rows], d)
    h = hid[...]
    for tap in range(9):
        block = lax.dot_general(
            h, cols[:, (8 - tap) * d.c : (9 - tap) * d.c], (((0,), (0,)), ((), ())), preferred_element_type=F32
        ) * factor
        at = tap * d.c
        while at < (tap + 1) * d.c:
            owner = at // chunk
            stop = min((owner + 1) * chunk, (tap + 1) * d.c)
            where = pl.ds(at - owner * chunk, stop - at)
            away = (positions[owner] - here + n) % n
            for i in range(2):
                piece = block[at - tap * d.c : stop - tap * d.c, i * LANES : (i + 1) * LANES]
                if not first:
                    piece = piece + before[i][away, where, :]
                halves[i][away, where, :] = piece
            at = stop
    for i, ref in enumerate(first_short):
        ref[...] = halves[i][(n // 2 + 1, n // 2 - 1)[i]]


def cost(weight):
    return pl.CostEstimate(flops=weight * 10**9, bytes_accessed=0, transcendentals=0)


VMEM = pl.BlockSpec(memory_space=pltpu.VMEM)
HBM = pl.BlockSpec(memory_space=pltpu.HBM)
SMEM = pl.BlockSpec(memory_space=pltpu.SMEM)
ANY = pl.BlockSpec(memory_space=pl.ANY)


class Chain:
    def __init__(self, chips, every):
        self.chips, self.every = chips, every
        self.tokens = []
        self.kept = {}

    def call(
        self,
        body,
        out_shape,
        scratch,
        weight,
        *operands,
        in_specs=None,
        alias=None,
        vmem=VMEM_LIMIT,
        follows=True,
        passed=(),
        stores=(),
        own=None,
    ):
        tokens = self.tokens if follows else []
        names = sorted({s[0] for s in stores} | ({own[0]} if own else set()))
        sources = [v for s in stores for v in s[2]]
        old = [self.kept[k] for k in names if k in self.kept]
        counts = [len(tokens), len(operands), len(passed), len(sources), len(old), 1, len(out_shape), len(passed), len(names)]
        starts = [sum(counts[:i]) for i in range(len(counts) + 1)]

        def chained(*refs):
            groups = [refs[starts[i] : starts[i + 1]] for i in range(len(counts))]
            rest = refs[starts[-1] :]
            outs, kept = groups[6], dict(zip(names, groups[8]))
            waits = []

            def send(source, name, tick, sem):
                copy = pltpu.make_async_copy(source, kept[name].at[tick], sem)
                copy.start()
                return copy

            if names:
                *rest, sems = rest
                from_refs = list(groups[3])
                for i, (name, tick, per_chip) in enumerate(stores):
                    mine, from_refs = from_refs[: len(per_chip)], from_refs[len(per_chip) :]
                    if len(mine) == 1:
                        waits.append(send(mine[0], name, tick, sems.at[i]))
                        continue
                    for c in range(len(mine)):

                        @pl.when(chip() == c)
                        def _():
                            send(mine[c], name, tick, sems.at[i])

                    waits.append(pltpu.make_async_copy(mine[0], kept[name].at[tick], sems.at[i]))
            total = jnp.zeros((8, LANES), F32)
            for ref in groups[0]:
                total = total + ref[...]
            groups[5][0][...] = total
            body(*groups[1], *outs, *rest)
            if own:
                name, tick, where = own
                if where is None:
                    waits.append(send((outs or rest)[0], name, tick, sems.at[len(stores)]))
                else:

                    @pl.when(chip() == where)
                    def _():
                        send(outs[0], name, tick, sems.at[len(stores)]).wait()

            for copy in waits:
                copy.wait()

        aliases = {starts[1] + i: starts[6] - starts[5] + o for i, o in (alias or {}).items()}
        aliases |= {starts[2] + i: 1 + len(out_shape) + i for i in range(len(passed))}
        aliases |= {
            starts[4] + i: 1 + len(out_shape) + len(passed) + names.index(k)
            for i, k in enumerate([k for k in names if k in self.kept])
        }
        token, *outs = pl.pallas_call(
            chained,
            out_shape=(
                jax.ShapeDtypeStruct((8, LANES), F32),
                *out_shape,
                *[jax.ShapeDtypeStruct(v.shape, v.dtype) for v in passed],
                *[self.every] * len(names),
            ),
            in_specs=[VMEM] * len(tokens)
            + (in_specs or [VMEM] * len(operands))
            + [VMEM] * len(passed)
            + [ANY] * (len(sources) + len(old)),
            out_specs=[VMEM] * (1 + len(out_shape) + len(passed)) + [ANY] * len(names),
            scratch_shapes=[*scratch] + ([pltpu.SemaphoreType.DMA((len(stores) + 1,))] if names else []),
            compiler_params=pltpu.CompilerParams(vmem_limit_bytes=vmem),
            cost_estimate=cost(weight),
            input_output_aliases=aliases,
        )(*tokens, *operands, *passed, *sources, *old)
        self.tokens = [token] if follows else self.tokens + [token]
        for k, v in zip(names, outs[len(out_shape) + len(passed) :]):
            self.kept[k] = v
        return outs[: len(out_shape) + len(passed)]


def add_kernel(up_offset, down_offset, first_terms, second_terms, first, second, first_out, second_out):
    first_out[...] = first_terms[up_offset] + first[...]
    second_out[...] = second_terms[down_offset] + second[...]


def final_kernel(first_terms, second_terms, first_up, first_down, second_down, second_up, out):
    out[:, :LANES] = first_terms[0] + first_up[...] + first_down[...]
    out[:, LANES:] = second_terms[0] + second_up[...] + second_down[...]


def shards(
    arriving_activations,
    fresh_images,
    saved_inputs,
    arriving_gradients,
    fresh_gradients,
    feed_order,
    forward_weight,
    forward_gain,
    forward_bias,
    backward_weight,
    backward_gain,
    backward_bias,
):
    ticks = saved_inputs.shape[0]
    d = Dims(*saved_inputs.shape[2:])
    sections = lax.axis_size("section")
    chips = sections // 2
    ring = [(i, (i + 1) % sections) for i in range(sections)]
    inside = [(i, i ^ 1) for i in range(sections)]

    act0 = interleaved(arriving_activations, d)
    grad0 = interleaved(arriving_gradients, d)
    fresh_act = interleaved(fresh_images, d)
    fresh_grad = interleaved(fresh_gradients, d)
    saved = interleaved(saved_inputs[:, 0], d)
    feed = feed_order.reshape(1, -1)
    fgain, fbias, bgain, bbias = [
        v[0].reshape(d.cts, LANES) for v in (forward_gain, forward_bias, backward_gain, backward_bias)
    ]

    msg = jax.ShapeDtypeStruct((d.flat, LANES), F32)
    every = jax.ShapeDtypeStruct((ticks, d.flat, LANES), F32)
    rows = d.n * d.pix
    wide = jax.ShapeDtypeStruct((rows, d.c), F32)
    padded = pltpu.VMEM((d.padded, LANES), F32)
    cols = pltpu.VMEM((rows, 9 * d.c), BF16)
    flat = pltpu.VMEM((d.flat, LANES), F32)
    sem = pltpu.SemaphoreType.DMA

    whole = pltpu.VMEM((rows, d.c), F32)
    vector = pltpu.VMEM((d.cts, LANES), F32)
    narrow = jax.ShapeDtypeStruct((rows, d.c), BF16)
    raw = pltpu.VMEM((d.flat, LANES), BF16)

    last = ticks - 1

    def later(shape, dtype):
        return jax.ShapeDtypeStruct((last, *shape), dtype)

    chain = Chain(chips, every)

    def first():
        return chain.call(
            functools.partial(first_kernel, d),
            (msg, narrow),
            [raw, raw, vector, vector, pltpu.VMEM(backward_weight.shape[1:], BF16), whole, whole, flat]
            + [padded] * 3
            + [cols, sem((5,))],
            0,
            saved,
            grad0,
            bgain,
            bbias,
            backward_weight[0],
            in_specs=[HBM] * 5,
            vmem=WHOLE_VMEM,
        )

    def prep(slot):
        return chain.call(
            functools.partial(prep_kernel, d, slot),
            (wide, wide, jax.ShapeDtypeStruct((8, LANES), F32), narrow),
            [flat],
            0,
            saved,
            bgain,
            bbias,
        )

    def backward(slot, slope, normed, rstd, **more):
        return chain.call(
            functools.partial(backward_kernel, d, slot),
            (msg, msg),
            [padded] * 3 + [cols],
            0,
            feed,
            fresh_grad,
            *arrivals(slot),
            slope,
            normed,
            rstd,
            backward_weight[0],
            **more,
        )

    def forward(t, arrived, **more):
        return chain.call(
            functools.partial(forward_kernel, d, t),
            (msg,) if t < last else (),
            [flat] * (t == last) + [padded] * 3 + [cols, flat],
            0,
            feed,
            fresh_act if t else act0,
            arrived,
            fgain,
            fbias,
            forward_weight[0],
            **more,
        )

    n = lax.axis_size("dp")
    order = list(range(0, n, 2)) + list(range(n - 1 - n % 2, 0, -2))
    positions = [order.index(i) for i in range(n)]
    chunk = 9 * d.c // n
    half = jax.ShapeDtypeStruct((n, chunk, LANES), F32)
    piece = jax.ShapeDtypeStruct((chunk, LANES), F32)

    def weight_terms(ticks, arrived, *before):
        used = sorted({t + c if t else 0 for t in ticks for c in range(chips)})
        operands = [hidden[k] for k in used]
        operands += [entered[k] if 0 < k < len(entered) else grad0 for k in used]
        return chain.call(
            functools.partial(weight_kernel, d, ticks, not before, chips, n, positions, 1.0 / (n * d.n), used),
            (half,) * 2 + ((piece,) * 2 if before else ()),
            [flat]
            + [padded] * 3
            + [pltpu.VMEM((len(ticks) * rows, 9 * d.c), BF16), pltpu.VMEM((len(ticks) * rows, d.c), BF16)],
            0,
            grad0,
            feed,
            fresh_grad,
            *arrived,
            *operands,
            *before,
            alias={7 + len(operands) + i: i for i in range(len(before))},
        )

    slots = ticks + chips - 1
    out, h = first()
    chain.tokens = []
    gradients, hidden, entered, inner, outer, outputs = [out], [h], [None], [], [], []

    def arrivals(slot):
        within = inner[0], inner[slot - 1]
        between = (outer[0], outer[max(slot - 2, 0)]) if slot > 1 else (inner[0], inner[0])
        return *within, *between

    prepared = [None]
    for slot in range(slots - 1):
        if slot > 0:
            out, e = backward(slot, *prepared[slot])
            gradients.append(out)
            entered.append(e)
        inner.append(lax.ppermute(gradients[slot], "section", inside))
        if slot < slots - 2:
            outer.append(lax.ppermute(gradients[slot], "section", ring))
            for later in [slot + 1] if slot < slots - 3 else [slot + 1, slot + 2]:
                *ready, h = prep(later)
                prepared.append(ready)
                hidden.append(h)
    terms = weight_terms(range(last), (inner[0],) * 4)
    *terms, short0, short1 = weight_terms([last], arrivals(slots - 1), *terms)

    onward = [(order[i], order[(i + 1) % n]) for i in range(n)]
    back = [(b, a) for a, b in onward]
    hops = n // 2

    def swapped(first, second, ways):
        return [lax.ppermute(v, "dp", way) for v, way in zip((first, second), ways)]

    def long_hop(pair):
        return swapped(*pair, (onward, back))

    def short_hop(pair):
        return swapped(*pair, (back, onward))

    def added(pair, up, down, weight):
        return chain.call(
            functools.partial(add_kernel, up % n, down % n), (piece,) * 2, [], weight, *terms, *pair
        )

    def returned(t):
        return ("returned", t, gradients[t : t + chips] if t else gradients[:1])

    def emitted(t):
        return ("emitted", t, outputs[t : t + 1])

    def forward_step(t, arrived, **more):
        out, *passed = forward(t, arrived, **more)
        outputs.append(out)
        return lax.ppermute(out, "section", ring), passed

    long = long_hop([terms[0][hops], terms[1][n - hops]])
    arrived, short = forward_step(0, inner[0], stores=[returned(0)], passed=[short0, short1])
    short = short_hop(short)
    for hop in range(1, hops):
        long = long_hop(added(long, hops - hop, hop - hops, 3))
        if hop < last and hop in ():
            arrived, _ = forward_step(hop, arrived, stores=[emitted(hop - 1), returned(hop)])
        if hop == 1:
            out, _ = backward(slots - 1, *prepared[slots - 1])
            gradients.append(out)
        if hop < hops - 1:
            short = short_hop(added(short, hop + 1 - hops, hops - 1 - hop, 3))
        if hop < last:
            arrived, _ = forward_step(hop, arrived, stores=[emitted(hop - 1), returned(hop)])
    forward(last, arrived, stores=[returned(last), emitted(last - 1)], own=("emitted", last, None))
    (shard_sum,) = chain.call(
        final_kernel, (jax.ShapeDtypeStruct((chunk, d.c), F32),), [], 0, *terms, *long[:1], *short[:1], *long[1:], *short[1:]
    )
    return (
        standard(chain.kept["emitted"], d)[:, None],
        standard(chain.kept["returned"], d)[:, None],
        shard_sum[None],
    )


def solution(mesh):
    placed = (
        P("section", "dp", None, None, None),
        P(None, "dp", None, None, None),
        P(None, "section", "dp", None, None, None),
        P("section", "dp", None, None, None),
        P(None, "dp", None, None, None),
        P(),
        P("section", None, None),
        P("section", None),
        P("section", None),
        P("section", None, None),
        P("section", None),
        P("section", None),
    )
    return jax.shard_map(
        shards,
        mesh=mesh,
        in_specs=placed,
        out_specs=(
            P(None, "section", "dp", None, None, None),
            P(None, "section", "dp", None, None, None),
            P("section", "dp", None),
        ),
        check_vma=False,
    )
```

```python
import functools
import math

import jax
import jax.numpy as jnp
from jax import lax
from jax.experimental import pallas as pl
from jax.experimental.pallas import tpu as pltpu
from jax.sharding import PartitionSpec as P

GROUPS = 32
F32 = jnp.float32
BF16 = jnp.bfloat16
LANES = 128
VMEM_LIMIT = 24 * 1024 * 1024
WHOLE_VMEM = 60 * 1024 * 1024


class Dims:
    def __init__(self, images, rows, cols, channels):
        self.n, self.h, self.w, self.c = images, rows, cols, channels
        self.cts = channels // LANES
        self.unit = self.cts * images
        self.pix = rows * cols
        self.flat = self.pix * self.unit
        per = 8 // math.gcd(8, self.unit)
        self.pad = -(-(cols + 1) // per) * per
        self.padded = (self.pix + 2 * self.pad) * self.unit
        self.count = self.pix * (channels // GROUPS)


def interleaved(x, d):
    lead = x.shape[:-4]
    k = len(lead)
    x = x.reshape(*lead, d.n, d.pix, d.cts, LANES)
    x = x.transpose(*range(k), k + 1, k + 2, k, k + 3)
    return x.reshape(*lead, d.flat, LANES)


def standard(x, d):
    lead = x.shape[:-2]
    k = len(lead)
    x = x.reshape(*lead, d.pix, d.cts, d.n, LANES)
    x = x.transpose(*range(k), k + 2, k, k + 1, k + 3)
    return x.reshape(*lead, d.n, d.h, d.w, d.c)


def group_sum(v, width):
    lane = lax.broadcasted_iota(jnp.int32, v.shape, 1)
    k = 1
    while k < width:
        v = v + jnp.where((lane & k) == 0, pltpu.roll(v, LANES - k, 1), pltpu.roll(v, k, 1))
        k *= 2
    return v


def pattern(ref, d):
    row = lax.broadcasted_iota(jnp.int32, (8, LANES), 0)
    ct = (row // d.n) % d.cts
    out = jnp.broadcast_to(ref[0:1, :], (8, LANES))
    for i in range(1, d.cts):
        out = jnp.where(ct == i, jnp.broadcast_to(ref[i : i + 1, :], (8, LANES)), out)
    return out


def unit_sum(v, d):
    s = jnp.sum(v, axis=0)
    k = d.unit
    while k < 8:
        s = s + pltpu.roll(s, k, 0)
        k *= 2
    return group_sum(s, d.c // GROUPS)


def normalized(x, d):
    tiles = x.reshape(-1, 8, LANES)
    scale = 1.0 / d.count
    mean = unit_sum(tiles, d) * scale
    centred = tiles - mean
    var = unit_sum(centred * centred, d) * scale
    rstd = lax.rsqrt(var + 1e-05)
    return centred * rstd, rstd


def sigmoid(a):
    return 0.5 * jnp.tanh(0.5 * a) + 0.5


def spread(value, refs, d):
    zeros = jnp.zeros((d.pad * d.unit, LANES), F32)
    for ref in refs:
        ref[0 : d.pad * d.unit, :] = zeros
        ref[d.padded - d.pad * d.unit : d.padded, :] = zeros
        ref[d.pad * d.unit : d.pad * d.unit + d.flat, :] = value
    edge = jnp.zeros((d.unit, LANES), F32)
    for i in range(d.h):
        last = (d.pad + i * d.w + d.w - 1) * d.unit
        first = (d.pad + i * d.w) * d.unit
        refs[0][last : last + d.unit, :] = edge
        refs[2][first : first + d.unit, :] = edge


def plane(ref, d, shift, n):
    parts = [
        ref[pl.ds((d.pad + shift) * d.unit + ct * d.n + n, d.pix, stride=d.unit), :] for ct in range(d.cts)
    ]
    return jnp.concatenate(parts, axis=1)


def gather_patches(refs, out_ref, d):
    for kr in range(3):
        for kc in range(3):
            tap = kr * 3 + kc
            for n in range(d.n):
                block = plane(refs[kc], d, (kr - 1) * d.w + kc - 1, n)
                out_ref[n * d.pix : (n + 1) * d.pix, tap * d.c : (tap + 1) * d.c] = block.astype(BF16)


def from_interleaved(ref, d, base=0):
    rows = [
        jnp.concatenate(
            [ref[pl.ds(base + ct * d.n + n, d.pix, stride=d.unit), :] for ct in range(d.cts)], axis=1
        )
        for n in range(d.n)
    ]
    return jnp.concatenate(rows, axis=0)


def to_interleaved(ref, n, value, d):
    for ct in range(d.cts):
        ref[pl.ds(ct * d.n + n, d.pix, stride=d.unit), :] = value[:, ct * LANES : (ct + 1) * LANES]


def prepare(d, x, gain_ref, bias_ref, slope_ref, normed_ref, hidden_ref, tmp):
    normed, rstd = normalized(x, d)
    gain = pattern(gain_ref, d)
    a = normed * gain + pattern(bias_ref, d)
    s = sigmoid(a)
    for ref, value in (
        (normed_ref, normed),
        (slope_ref, s * (1.0 + a * (1.0 - s)) * gain),
        (hidden_ref, a * s),
    ):
        tmp[...] = value.reshape(d.flat, LANES)
        ref[...] = from_interleaved(tmp, d).astype(ref.dtype)
    return rstd


def prep_kernel(d, slot, saved_ref, gain_ref, bias_ref, slope_ref, normed_ref, rstd_ref, hidden_ref, tmp):
    tick = slot - chip()
    last = saved_ref.shape[0] - 1

    @pl.when(jnp.logical_and(tick >= 1, tick <= last))
    def _():
        x = saved_ref[jnp.minimum(jnp.maximum(tick, 1), last)].astype(F32)
        rstd_ref[...] = prepare(d, x, gain_ref, bias_ref, slope_ref, normed_ref, hidden_ref, tmp)


def picked(feed_ref, tick, fresh_ref):
    index = feed_ref[:, tick - 1 : tick]
    out = fresh_ref[0].astype(F32)
    for k in range(1, fresh_ref.shape[0]):
        out = jnp.where(index == k, fresh_ref[k].astype(F32), out)
    return out


def through_layer(d, cols, weight_ref, slope_ref, normed_ref, rstd, mid, out_ref):
    grad = None
    for tap in range(9):
        part = lax.dot_general(
            cols[:, tap * d.c : (tap + 1) * d.c],
            weight_ref[(8 - tap) * d.c : (9 - tap) * d.c, :],
            (((1,), (1,)), ((), ())),
            preferred_element_type=F32,
        )
        grad = part if grad is None else grad + part
    through = grad * slope_ref[...]
    weighted = through * normed_ref[...]
    rows = []
    for ct in range(d.cts):
        for n in range(d.n):
            for v in (through, weighted):
                rows.append(
                    jnp.sum(v[n * d.pix : (n + 1) * d.pix, ct * LANES : (ct + 1) * LANES], axis=0, keepdims=True)
                )
    sums = group_sum(jnp.concatenate(rows, axis=0), d.c // GROUPS) * (1.0 / d.count)
    for n in range(d.n):
        for ct in range(d.cts):
            where = ct * d.n + n
            k = where * 2
            here = (slice(n * d.pix, (n + 1) * d.pix), slice(ct * LANES, (ct + 1) * LANES))
            value = (through[here] - sums[k : k + 1] - normed_ref[here] * sums[k + 1 : k + 2]) * rstd[where : where + 1, :]
            e_here = mid[pl.ds(d.pad * d.unit + where, d.pix, stride=d.unit), :]
            out_ref[pl.ds(where, d.pix, stride=d.unit), :] = value + e_here


def first_kernel(d, saved_hbm, grad_hbm, gain_hbm, bias_hbm, weight_hbm, *refs):
    out_ref, hidden, saved, grad, gain, bias, weight, slope, normed, tmp, left, mid, right, cols, sems = refs
    pairs = [(grad_hbm.at[0], grad), (saved_hbm.at[0], saved), (gain_hbm, gain), (bias_hbm, bias), (weight_hbm, weight)]
    copies = [pltpu.make_async_copy(src, dst, sems.at[i]) for i, (src, dst) in enumerate(pairs)]
    for copy in copies:
        copy.start()
    copies[0].wait()
    spread(grad[...].astype(F32), (left, mid, right), d)
    gather_patches((left, mid, right), cols, d)
    for copy in copies[1:4]:
        copy.wait()
    rstd = prepare(d, saved[...].astype(F32), gain, bias, slope, normed, hidden, tmp)
    copies[4].wait()
    through_layer(d, cols, weight, slope, normed, rstd, mid, out_ref)


def chip():
    return lax.axis_index("section") // 2


def enter(slot, feed_ref, fresh_ref, inner0_ref, inner_ref, outer0_ref, outer_ref, e_ref):
    tick = slot - chip()
    second = lax.axis_index("section") % 2 == 1
    beyond = jnp.logical_and(jnp.logical_not(second), chip() > 0)

    for condition, ref in (
        (jnp.logical_and(second, tick == 1), inner0_ref),
        (jnp.logical_and(second, tick > 1), inner_ref),
        (jnp.logical_and(beyond, tick == 1), outer0_ref),
        (jnp.logical_and(beyond, tick > 1), outer_ref),
    ):

        @pl.when(condition)
        def _():
            e_ref[...] = ref[...]

    if slot <= feed_ref.shape[1]:

        @pl.when(lax.axis_index("section") == 0)
        def _():
            e_ref[...] = picked(feed_ref, slot, fresh_ref)


def backward_kernel(d, slot, feed_ref, fresh_ref, *refs):
    arrived, (slope_ref, normed_ref, rstd_ref, weight_ref), refs = refs[:4], refs[4:8], refs[8:]
    out_ref, e_ref, left, mid, right, cols = refs
    tick = slot - chip()
    runs = jnp.logical_and(tick >= 1, tick <= feed_ref.shape[1])

    @pl.when(runs)
    def _():
        enter(slot, feed_ref, fresh_ref, *arrived, e_ref)
        spread(e_ref[...], (left, mid, right), d)
        gather_patches((left, mid, right), cols, d)
        through_layer(d, cols, weight_ref, slope_ref, normed_ref, rstd_ref[...], mid, out_ref)

    @pl.when(jnp.logical_not(runs))
    def _():
        out_ref[...] = jnp.zeros_like(out_ref)
        e_ref[...] = jnp.zeros_like(e_ref)


def forward_kernel(d, tick, feed_ref, fresh_ref, arrived_ref, gain_ref, bias_ref, weight_ref, *refs):
    out_ref, left, mid, right, cols, kept = refs
    if tick == 0:
        x = fresh_ref[0].astype(F32)
        kept[...] = x
    else:
        section = lax.axis_index("section")

        @pl.when(section == 0)
        def _():
            kept[...] = picked(feed_ref, tick, fresh_ref)

        @pl.when(section != 0)
        def _():
            kept[...] = arrived_ref[...]

        x = kept[...]
    normed, _ = normalized(x, d)
    a = normed * pattern(gain_ref, d) + pattern(bias_ref, d)
    hidden = (a * sigmoid(a)).reshape(d.flat, LANES)
    spread(hidden, (left, mid, right), d)
    gather_patches((left, mid, right), cols, d)
    conv = jnp.dot(cols[...], weight_ref[...], preferred_element_type=F32)
    for n in range(d.n):
        for ct in range(d.cts):
            where = pl.ds(ct * d.n + n, d.pix, stride=d.unit)
            out_ref[where, :] = (
                kept[where, :] + conv[n * d.pix : (n + 1) * d.pix, ct * LANES : (ct + 1) * LANES]
            )


def weight_kernel(d, ticks, first, chips, n, positions, factor, slots, grad0_ref, feed_ref, fresh_ref, *refs):
    me = lax.axis_index("dp")
    here = jnp.where(me % 2 == 0, me // 2, n - 1 - me // 2)
    rows = d.n * d.pix
    chunk = 9 * d.c // n
    last = feed_ref.shape[1]
    arrived, refs = refs[:4], refs[4:]
    hidden_refs, refs = dict(zip(slots, refs)), refs[len(slots) :]
    e_refs, refs = dict(zip(slots, refs)), refs[len(slots) :]
    before, refs = (None, refs) if first else (refs[:2], refs[2:])
    halves, first_short, (kept, left, mid, right, cols, hid) = refs[:2], refs[2:-6], refs[-6:]
    for i, t in enumerate(ticks):
        if t == 0:
            kept[...] = grad0_ref[0].astype(F32)
            hid[i * rows : (i + 1) * rows, :] = hidden_refs[0][...]
        for c in range(chips if t else 0):

            @pl.when(chip() == c)
            def _():
                hid[i * rows : (i + 1) * rows, :] = hidden_refs[t + c][...]
                if t + c == last + chips - 1:
                    enter(t + c, feed_ref, fresh_ref, *arrived, kept)
                else:
                    kept[...] = e_refs[t + c][...]

        spread(kept[...], (left, mid, right), d)
        gather_patches((left, mid, right), cols.at[i * rows : (i + 1) * rows], d)
    h = hid[...]
    for tap in range(9):
        block = lax.dot_general(
            h, cols[:, (8 - tap) * d.c : (9 - tap) * d.c], (((0,), (0,)), ((), ())), preferred_element_type=F32
        ) * factor
        at = tap * d.c
        while at < (tap + 1) * d.c:
            owner = at // chunk
            stop = min((owner + 1) * chunk, (tap + 1) * d.c)
            where = pl.ds(at - owner * chunk, stop - at)
            away = (positions[owner] - here + n) % n
            for i in range(2):
                piece = block[at - tap * d.c : stop - tap * d.c, i * LANES : (i + 1) * LANES]
                if not first:
                    piece = piece + before[i][away, where, :]
                halves[i][away, where, :] = piece
            at = stop
    for i, ref in enumerate(first_short):
        ref[...] = halves[i][(n // 2 + 1, n // 2 - 1)[i]]


def cost(weight):
    return pl.CostEstimate(flops=weight * 10**9, bytes_accessed=0, transcendentals=0)


VMEM = pl.BlockSpec(memory_space=pltpu.VMEM)
HBM = pl.BlockSpec(memory_space=pltpu.HBM)
SMEM = pl.BlockSpec(memory_space=pltpu.SMEM)
ANY = pl.BlockSpec(memory_space=pl.ANY)


class Chain:
    def __init__(self, chips, every):
        self.chips, self.every = chips, every
        self.tokens = []
        self.kept = {}

    def call(
        self,
        body,
        out_shape,
        scratch,
        weight,
        *operands,
        in_specs=None,
        alias=None,
        vmem=VMEM_LIMIT,
        follows=True,
        passed=(),
        stores=(),
        own=None,
    ):
        tokens = self.tokens if follows else []
        names = sorted({s[0] for s in stores} | ({own[0]} if own else set()))
        sources = [v for s in stores for v in s[2]]
        old = [self.kept[k] for k in names if k in self.kept]
        counts = [len(tokens), len(operands), len(passed), len(sources), len(old), 1, len(out_shape), len(passed), len(names)]
        starts = [sum(counts[:i]) for i in range(len(counts) + 1)]

        def chained(*refs):
            groups = [refs[starts[i] : starts[i + 1]] for i in range(len(counts))]
            rest = refs[starts[-1] :]
            outs, kept = groups[6], dict(zip(names, groups[8]))
            waits = []

            def send(source, name, tick, sem):
                copy = pltpu.make_async_copy(source, kept[name].at[tick], sem)
                copy.start()
                return copy

            if names:
                *rest, sems = rest
                from_refs = list(groups[3])
                for i, (name, tick, per_chip) in enumerate(stores):
                    mine, from_refs = from_refs[: len(per_chip)], from_refs[len(per_chip) :]
                    if len(mine) == 1:
                        waits.append(send(mine[0], name, tick, sems.at[i]))
                        continue
                    for c in range(len(mine)):

                        @pl.when(chip() == c)
                        def _():
                            send(mine[c], name, tick, sems.at[i])

                    waits.append(pltpu.make_async_copy(mine[0], kept[name].at[tick], sems.at[i]))
            total = jnp.zeros((8, LANES), F32)
            for ref in groups[0]:
                total = total + ref[...]
            groups[5][0][...] = total
            body(*groups[1], *outs, *rest)
            if own:
                name, tick, where = own
                if where is None:
                    waits.append(send((outs or rest)[0], name, tick, sems.at[len(stores)]))
                else:

                    @pl.when(chip() == where)
                    def _():
                        send(outs[0], name, tick, sems.at[len(stores)]).wait()

            for copy in waits:
                copy.wait()

        aliases = {starts[1] + i: starts[6] - starts[5] + o for i, o in (alias or {}).items()}
        aliases |= {starts[2] + i: 1 + len(out_shape) + i for i in range(len(passed))}
        aliases |= {
            starts[4] + i: 1 + len(out_shape) + len(passed) + names.index(k)
            for i, k in enumerate([k for k in names if k in self.kept])
        }
        token, *outs = pl.pallas_call(
            chained,
            out_shape=(
                jax.ShapeDtypeStruct((8, LANES), F32),
                *out_shape,
                *[jax.ShapeDtypeStruct(v.shape, v.dtype) for v in passed],
                *[self.every] * len(names),
            ),
            in_specs=[VMEM] * len(tokens)
            + (in_specs or [VMEM] * len(operands))
            + [VMEM] * len(passed)
            + [ANY] * (len(sources) + len(old)),
            out_specs=[VMEM] * (1 + len(out_shape) + len(passed)) + [ANY] * len(names),
            scratch_shapes=[*scratch] + ([pltpu.SemaphoreType.DMA((len(stores) + 1,))] if names else []),
            compiler_params=pltpu.CompilerParams(vmem_limit_bytes=vmem),
            cost_estimate=cost(weight),
            input_output_aliases=aliases,
        )(*tokens, *operands, *passed, *sources, *old)
        self.tokens = [token] if follows else self.tokens + [token]
        for k, v in zip(names, outs[len(out_shape) + len(passed) :]):
            self.kept[k] = v
        return outs[: len(out_shape) + len(passed)]


def add_kernel(up_offset, down_offset, first_terms, second_terms, first, second, first_out, second_out):
    first_out[...] = first_terms[up_offset] + first[...]
    second_out[...] = second_terms[down_offset] + second[...]


def final_kernel(first_terms, second_terms, first_up, first_down, second_down, second_up, out):
    out[:, :LANES] = first_terms[0] + first_up[...] + first_down[...]
    out[:, LANES:] = second_terms[0] + second_up[...] + second_down[...]


def shards(
    arriving_activations,
    fresh_images,
    saved_inputs,
    arriving_gradients,
    fresh_gradients,
    feed_order,
    forward_weight,
    forward_gain,
    forward_bias,
    backward_weight,
    backward_gain,
    backward_bias,
):
    ticks = saved_inputs.shape[0]
    d = Dims(*saved_inputs.shape[2:])
    sections = lax.axis_size("section")
    chips = sections // 2
    ring = [(i, (i + 1) % sections) for i in range(sections)]
    inside = [(i, i ^ 1) for i in range(sections)]

    act0 = interleaved(arriving_activations, d)
    grad0 = interleaved(arriving_gradients, d)
    fresh_act = interleaved(fresh_images, d)
    fresh_grad = interleaved(fresh_gradients, d)
    saved = interleaved(saved_inputs[:, 0], d)
    feed = feed_order.reshape(1, -1)
    fgain, fbias, bgain, bbias = [
        v[0].reshape(d.cts, LANES) for v in (forward_gain, forward_bias, backward_gain, backward_bias)
    ]

    msg = jax.ShapeDtypeStruct((d.flat, LANES), F32)
    every = jax.ShapeDtypeStruct((ticks, d.flat, LANES), F32)
    rows = d.n * d.pix
    wide = jax.ShapeDtypeStruct((rows, d.c), F32)
    padded = pltpu.VMEM((d.padded, LANES), F32)
    cols = pltpu.VMEM((rows, 9 * d.c), BF16)
    flat = pltpu.VMEM((d.flat, LANES), F32)
    sem = pltpu.SemaphoreType.DMA

    whole = pltpu.VMEM((rows, d.c), F32)
    vector = pltpu.VMEM((d.cts, LANES), F32)
    narrow = jax.ShapeDtypeStruct((rows, d.c), BF16)
    raw = pltpu.VMEM((d.flat, LANES), BF16)

    last = ticks - 1

    def later(shape, dtype):
        return jax.ShapeDtypeStruct((last, *shape), dtype)

    chain = Chain(chips, every)

    def first():
        return chain.call(
            functools.partial(first_kernel, d),
            (msg, narrow),
            [raw, raw, vector, vector, pltpu.VMEM(backward_weight.shape[1:], BF16), whole, whole, flat]
            + [padded] * 3
            + [cols, sem((5,))],
            0,
            saved,
            grad0,
            bgain,
            bbias,
            backward_weight[0],
            in_specs=[HBM] * 5,
            vmem=WHOLE_VMEM,
        )

    def prep(slot):
        return chain.call(
            functools.partial(prep_kernel, d, slot),
            (wide, wide, jax.ShapeDtypeStruct((8, LANES), F32), narrow),
            [flat],
            0,
            saved,
            bgain,
            bbias,
        )

    def backward(slot, slope, normed, rstd, **more):
        return chain.call(
            functools.partial(backward_kernel, d, slot),
            (msg, msg),
            [padded] * 3 + [cols],
            0,
            feed,
            fresh_grad,
            *arrivals(slot),
            slope,
            normed,
            rstd,
            backward_weight[0],
            **more,
        )

    def forward(t, arrived, **more):
        return chain.call(
            functools.partial(forward_kernel, d, t),
            (msg,) if t < last else (),
            [flat] * (t == last) + [padded] * 3 + [cols, flat],
            0,
            feed,
            fresh_act if t else act0,
            arrived,
            fgain,
            fbias,
            forward_weight[0],
            **more,
        )

    n = lax.axis_size("dp")
    order = list(range(0, n, 2)) + list(range(n - 1 - n % 2, 0, -2))
    positions = [order.index(i) for i in range(n)]
    chunk = 9 * d.c // n
    half = jax.ShapeDtypeStruct((n, chunk, LANES), F32)
    piece = jax.ShapeDtypeStruct((chunk, LANES), F32)

    def weight_terms(ticks, arrived, *before):
        used = sorted({t + c if t else 0 for t in ticks for c in range(chips)})
        operands = [hidden[k] for k in used]
        operands += [entered[k] if 0 < k < len(entered) else grad0 for k in used]
        return chain.call(
            functools.partial(weight_kernel, d, ticks, not before, chips, n, positions, 1.0 / (n * d.n), used),
            (half,) * 2 + ((piece,) * 2 if last in ticks else ()),
            [flat]
            + [padded] * 3
            + [pltpu.VMEM((len(ticks) * rows, 9 * d.c), BF16), pltpu.VMEM((len(ticks) * rows, d.c), BF16)],
            0,
            grad0,
            feed,
            fresh_grad,
            *arrived,
            *operands,
            *before,
            alias={7 + len(operands) + i: i for i in range(len(before))},
        )

    slots = ticks + chips - 1
    out, h = first()
    chain.tokens = []
    gradients, hidden, entered, inner, outer, outputs = [out], [h], [None], [], [], []

    def arrivals(slot):
        within = inner[0], inner[slot - 1]
        between = (outer[0], outer[max(slot - 2, 0)]) if slot > 1 else (inner[0], inner[0])
        return *within, *between

    prepared = [None]
    for slot in range(slots - 1):
        if slot > 0:
            out, e = backward(slot, *prepared[slot])
            gradients.append(out)
            entered.append(e)
        inner.append(lax.ppermute(gradients[slot], "section", inside))
        if slot < slots - 2:
            outer.append(lax.ppermute(gradients[slot], "section", ring))
            for later in [slot + 1] if slot < slots - 3 else [slot + 1, slot + 2]:
                *ready, h = prep(later)
                prepared.append(ready)
                hidden.append(h)
        if slot == slots - 4:
            terms = weight_terms([0], (inner[0],) * 4)
    terms = weight_terms(range(1, last), (inner[0],) * 4, *terms)
    *terms, short0, short1 = weight_terms([last], arrivals(slots - 1), *terms)

    onward = [(order[i], order[(i + 1) % n]) for i in range(n)]
    back = [(b, a) for a, b in onward]
    hops = n // 2

    def swapped(first, second, ways):
        return [lax.ppermute(v, "dp", way) for v, way in zip((first, second), ways)]

    def long_hop(pair):
        return swapped(*pair, (onward, back))

    def short_hop(pair):
        return swapped(*pair, (back, onward))

    def added(pair, up, down, weight):
        return chain.call(
            functools.partial(add_kernel, up % n, down % n), (piece,) * 2, [], weight, *terms, *pair
        )

    def returned(t):
        return ("returned", t, gradients[t : t + chips] if t else gradients[:1])

    def emitted(t):
        return ("emitted", t, outputs[t : t + 1])

    def forward_step(t, arrived, **more):
        out, *passed = forward(t, arrived, **more)
        outputs.append(out)
        return lax.ppermute(out, "section", ring), passed

    long = long_hop([terms[0][hops], terms[1][n - hops]])
    arrived, short = forward_step(0, inner[0], stores=[returned(0)], passed=[short0, short1])
    short = short_hop(short)
    for hop in range(1, hops):
        long = long_hop(added(long, hops - hop, hop - hops, 3))
        if hop == 1:
            out, _ = backward(slots - 1, *prepared[slots - 1])
            gradients.append(out)
        if hop < hops - 1:
            short = short_hop(added(short, hop + 1 - hops, hops - 1 - hop, 3))
        if hop < last:
            arrived, _ = forward_step(hop, arrived, stores=[emitted(hop - 1), returned(hop)])
    forward(last, arrived, stores=[returned(last), emitted(last - 1)], own=("emitted", last, None))
    (shard_sum,) = chain.call(
        final_kernel, (jax.ShapeDtypeStruct((chunk, d.c), F32),), [], 0, *terms, *long[:1], *short[:1], *long[1:], *short[1:]
    )
    return (
        standard(chain.kept["emitted"], d)[:, None],
        standard(chain.kept["returned"], d)[:, None],
        shard_sum[None],
    )


def solution(mesh):
    placed = (
        P("section", "dp", None, None, None),
        P(None, "dp", None, None, None),
        P(None, "section", "dp", None, None, None),
        P("section", "dp", None, None, None),
        P(None, "dp", None, None, None),
        P(),
        P("section", None, None),
        P("section", None),
        P("section", None),
        P("section", None, None),
        P("section", None),
        P("section", None),
    )
    return jax.shard_map(
        shards,
        mesh=mesh,
        in_specs=placed,
        out_specs=(
            P(None, "section", "dp", None, None, None),
            P(None, "section", "dp", None, None, None),
            P("section", "dp", None),
        ),
        check_vma=False,
    )
```
